32 devices in a mesh: row: 4 (over y, x), col: 8 (over z, core).
Axes of the slice: x: 2, y: 2, z: 4, core: 2. Of those that a mesh axis runs over, the one named last changes fastest.
Arguments:
- right_side: float32 [64, 20480], P(None, ('row', 'col')), may hold values from -6 to 6
- self_term: float32 [20480], P(('row', 'col')), may hold values from 1 to 4
- near_tiles: bfloat16 [4, 8, 32, 128, 128], P('row', 'col'), may hold values from -0.03125 to 0.03125
- near_rows: int32 [4, 8, 32], P('row', 'col'), may hold values from 0 to 39, as said below
- near_cols: int32 [4, 8, 32], P('row', 'col'), may hold values from 0 to 19, as said below
- near_count: int32 [4, 8], P('row', 'col'), may hold values from 8 to 32, as said below
- far_left: bfloat16 [4, 8, 64, 32, 128], P('row', 'col'), may hold values from -0.09375 to 0.09375
- far_right: bfloat16 [4, 8, 64, 32, 128], P('row', 'col'), may hold values from -0.09375 to 0.09375
- far_rows: int32 [4, 8, 64], P('row', 'col'), may hold values from 0 to 39, as said below
- far_cols: int32 [4, 8, 64], P('row', 'col'), may hold values from 0 to 19, as said below
- far_rank: int32 [4, 8, 64], P('row', 'col'), may hold values from 1 to 32
Outputs:
- solution: float32 [64, 20480], P(None, ('row', 'col'))
- residual: float32 [64, 20480], P(None, ('row', 'col'))
The draws below stay inside these ranges and needn't reach their ends.
Inputs may be any that keep to these rules, and one draw needn't show every extreme that they name: Slots 0 to near_count - 1 of a device's near-field lists hold tiles and the others are ignored; on some device all 32 slots are occupied. Factor rows from far_rank on of a far tile are ignored. On one device, the (near_rows, near_cols) and (far_rows, far_cols) pairs of all slots are distinct from one another. `near_cols`: see near_rows. `far_rows`: see near_rows. `far_cols`: see near_rows.
All inputs are finite; a program needn't handle non-finite values.
Results may differ from the reference program's by a relative error of at most 0.02.
Values may be sent and summed in bfloat16 or wider, within the bound.
No kernel may reach another device: no remote copies, remote signals or barrier semaphores. Data moves between devices by JAX's collectives and lax.ppermute only.
A program may use at most 64 MiB of HBM per device.

```python
import math
import jax
import jax.numpy as jnp
from jax import lax

LC = 64
CS = 128
KMAX = 32
ITERS = 3
CPD = 5
NEAR_DEV = 32
FAR_DEV = 64
RGC = 40
CGC = 20
NTOT = 20480
N_ROW = 4
N_COL = 8


def draw_near_count(key, part):
    first_key, second_key = jax.random.split(jax.random.fold_in(key, 7))
    divisor = jax.random.randint(first_key, (N_ROW * N_COL,), 1, 5)
    occupied = jnp.floor_divide(NEAR_DEV, divisor)
    chosen = jax.random.randint(second_key, (), 0, N_ROW * N_COL)
    occupied = occupied.at[chosen].set(NEAR_DEV)
    return occupied.reshape(N_ROW, N_COL).astype(jnp.int32)


def pair_lists(key):
    device_keys = jax.random.split(jax.random.fold_in(key, 11), N_ROW * N_COL)

    def one_device(device_key):
        return jax.random.permutation(device_key, RGC * CGC)
    return jax.vmap(one_device)(device_keys).astype(jnp.int32)


def draw_near_rows(key, part):
    pairs = pair_lists(key)[:, :NEAR_DEV]
    return (pairs // CGC).reshape(N_ROW, N_COL, NEAR_DEV).astype(jnp.int32)


def draw_near_cols(key, part):
    pairs = pair_lists(key)[:, :NEAR_DEV]
    return (pairs % CGC).reshape(N_ROW, N_COL, NEAR_DEV).astype(jnp.int32)


def draw_far_rows(key, part):
    pairs = pair_lists(key)[:, NEAR_DEV:NEAR_DEV + FAR_DEV]
    return (pairs // CGC).reshape(N_ROW, N_COL, FAR_DEV).astype(jnp.int32)


def draw_far_cols(key, part):
    pairs = pair_lists(key)[:, NEAR_DEV:NEAR_DEV + FAR_DEV]
    return (pairs % CGC).reshape(N_ROW, N_COL, FAR_DEV).astype(jnp.int32)


def plant(array, stream_key, low, largest):
    longest = array.shape.index(max(array.shape))
    spots = []
    for shift in (0, 1):
        where = [jax.random.randint(jax.random.fold_in(stream_key, axis), (), 0, length) for axis, length in enumerate(array.shape)]
        where[longest] = (where[longest] + shift) % array.shape[longest]
        spots.append(tuple(where))
    return array.at[spots[0]].set(low).at[spots[1]].set(largest)


def shard_levels(key, shape, pieces, smallest, top_value):
    def one(axis_at, parts):
        heights = jax.random.uniform(jax.random.fold_in(jax.random.fold_in(key, 6), axis_at), (parts,), jnp.float32, smallest / len(pieces), top_value / len(pieces))
        return jnp.repeat(jnp.exp(heights), shape[axis_at] // parts).reshape((-1,) + (1,) * (len(shape) - axis_at - 1))

    gain = one(*pieces[0])
    for cut in pieces[1:]:
        gain = gain * one(*cut)
    return gain


def gaussian(rng, dims, spread, bound, pieces=(), held_as=jnp.bfloat16):
    gain = shard_levels(rng, dims, pieces, -0.22, 0.18) if pieces else 1.0
    drawn = jax.random.normal(rng, dims, jnp.float32) * spread * gain
    return jnp.minimum(jnp.maximum(drawn, -bound), bound).astype(held_as)


def setup_inputs(seed: int = 0) -> dict:
    seeds = jax.random.split(jax.random.key(seed), 12)
    return {
        "right_side": gaussian(seeds[0], (LC, NTOT), 1.0, 6.0, ((1, 32),), jnp.float32),
        "self_term": jnp.clip(jnp.exp(math.log(4.0) - 1.3862944 * jax.random.uniform(seeds[1], (NTOT,), jnp.float32) ** shard_levels(seeds[1], (NTOT,), ((0, 32),), -0.2, 0.2)), 1.0, 4.0),
        "near_tiles": gaussian(seeds[2], (N_ROW, N_COL, NEAR_DEV, CS, CS), (8 * NEAR_DEV * CS) ** -0.5, 0.03125, ((0, 4), (1, 8))),
        "near_rows": draw_near_rows(jax.random.fold_in(seeds[11], 71), 0),
        "near_cols": draw_near_cols(jax.random.fold_in(seeds[11], 71), 0),
        "near_count": draw_near_count(jax.random.fold_in(seeds[11], 71), 0),
        "far_left": gaussian(seeds[6], (N_ROW, N_COL, FAR_DEV, KMAX, CS), (CS * KMAX) ** -0.5, 0.09375, ((0, 4), (1, 8))),
        "far_right": gaussian(seeds[7], (N_ROW, N_COL, FAR_DEV, KMAX, CS), (CS * KMAX) ** -0.5, 0.09375, ((0, 4), (1, 8))),
        "far_rows": draw_far_rows(jax.random.fold_in(seeds[11], 71), 0),
        "far_cols": draw_far_cols(jax.random.fold_in(seeds[11], 71), 0),
        "far_rank": plant(jax.random.randint(seeds[10], (N_ROW, N_COL, FAR_DEV), 1, KMAX + 1), jax.random.fold_in(seeds[10], 1), 1, KMAX).astype(jnp.int32),
    }


def small_solve(matrix, rhs):
    lower = jnp.linalg.cholesky(matrix)
    return jax.scipy.linalg.cho_solve((lower, True), rhs)

def inner_gram(left_rows, right_rows):
    return jnp.dot(left_rows.astype(jnp.float32), right_rows.T.astype(jnp.float32), preferred_element_type=jnp.float32, precision=lax.Precision.HIGHEST)

def combine_rows(weights, rows_in):
    return jnp.dot(weights.T.astype(jnp.float32), rows_in.astype(jnp.float32), preferred_element_type=jnp.float32, precision=lax.Precision.HIGHEST)

def round_kept(values):
    rounded = lax.optimization_barrier(values.astype(jnp.bfloat16))
    return rounded.astype(jnp.float32)

def reference(right_side, self_term, near_tiles, near_rows, near_cols, near_count, far_left, far_right, far_rows, far_cols, far_rank):
    clusters = CPD * N_ROW * N_COL
    slot_near = jnp.arange(NEAR_DEV, dtype=jnp.int32)
    rank_iota = jnp.arange(KMAX, dtype=jnp.int32)
    row_local = jnp.arange(RGC, dtype=jnp.int32)
    col_local = jnp.arange(CGC, dtype=jnp.int32)

    def operator(direction):
        cells = round_kept(direction).reshape(LC, clusters, CS)

        def per_device(total, device):
            grid_row = device // N_COL
            grid_col = device % N_COL

            def row_cluster(local):
                return ((grid_row * N_COL + local // CPD) * CPD + local % CPD).astype(jnp.int32)

            def col_cluster(local):
                return ((local // CPD * N_COL + grid_col) * CPD + local % CPD).astype(jnp.int32)
            row_total = jnp.zeros((LC, RGC, CS), jnp.float32)
            col_total = jnp.zeros((LC, CGC, CS), jnp.float32)
            tiles = near_tiles[grid_row, grid_col].astype(jnp.float32)
            near_p = near_rows[grid_row, grid_col]
            near_q = near_cols[grid_row, grid_col]
            live = (slot_near < near_count[grid_row, grid_col]).astype(jnp.float32)[None, :, None]
            to_rows = jnp.einsum('sij,lsj->lsi', tiles, cells[:, col_cluster(near_q)]) * live
            to_cols = jnp.einsum('sij,lsi->lsj', tiles, cells[:, row_cluster(near_p)]) * live
            row_total = row_total.at[:, near_p].add(to_rows)
            col_total = col_total.at[:, near_q].add(to_cols)
            left_f = far_left[grid_row, grid_col].astype(jnp.float32)
            right_f = far_right[grid_row, grid_col].astype(jnp.float32)
            far_p = far_rows[grid_row, grid_col]
            far_q = far_cols[grid_row, grid_col]
            keep = (rank_iota[None, :] < far_rank[grid_row, grid_col][:, None]).astype(jnp.float32)[None]
            coeff_q = round_kept(jnp.einsum('skj,lsj->lsk', right_f, cells[:, col_cluster(far_q)]) * keep)
            coeff_p = round_kept(jnp.einsum('ski,lsi->lsk', left_f, cells[:, row_cluster(far_p)]) * keep)
            row_total = row_total.at[:, far_p].add(jnp.einsum('ski,lsk->lsi', left_f, coeff_q))
            col_total = col_total.at[:, far_q].add(jnp.einsum('skj,lsk->lsj', right_f, coeff_p))
            total = total.at[:, row_cluster(row_local)].add(round_kept(row_total))
            total = total.at[:, col_cluster(col_local)].add(round_kept(col_total))
            return (total, None)
        total, _ = lax.scan(per_device, jnp.zeros((LC, clusters, CS), jnp.float32), jnp.arange(N_ROW * N_COL, dtype=jnp.int32))
        return self_term[None, :] * direction + total.reshape(LC, clusters * CS)
    solution = jnp.zeros_like(right_side)
    residual = right_side
    direction = right_side
    res_gram = inner_gram(residual, residual)
    for turn in range(ITERS):
        image = operator(direction)
        curvature = inner_gram(direction, image)
        alpha = small_solve(curvature, res_gram)
        solution = solution + combine_rows(alpha, direction)
        residual = residual - combine_rows(alpha, image)
        if turn + 1 < ITERS:
            new_gram = inner_gram(residual, residual)
            beta = small_solve(res_gram, new_gram)
            direction = residual + combine_rows(beta, direction)
            res_gram = new_gram
    return (solution, residual)
```

```python
import functools

import jax
import jax.numpy as jnp
from jax import lax
from jax.experimental import pallas as pl
from jax.experimental.pallas import tpu as pltpu
from jax.sharding import PartitionSpec as P

SHIFT = 2.5
VMEM_BYTES = 48 * 1024 * 1024
HIGHEST = lax.Precision.HIGHEST

vmem = pl.BlockSpec(memory_space=pltpu.VMEM)
smem = pl.BlockSpec(memory_space=pltpu.SMEM)
params = pltpu.CompilerParams(vmem_limit_bytes=VMEM_BYTES)


def f32(*shape):
    return jax.ShapeDtypeStruct(shape, jnp.float32)


def bf16(*shape):
    return jax.ShapeDtypeStruct(shape, jnp.bfloat16)


def contract(left, right, dims, precision=None):
    return lax.dot_general(
        left, right, (dims, ((), ())), precision=precision, preferred_element_type=jnp.float32
    )


def partner_permute(value, axis, flip):
    size = lax.axis_size(axis)
    return lax.ppermute(value, axis, [(i, i ^ flip) for i in range(size)])


def dense_kernel(count_ref, rank_ref, near_ref, left_ref, right_ref, tile_ref, turned_ref):
    near_slots, far_slots = near_ref.shape[0], left_ref.shape[0]

    def near(s, _):
        tile = near_ref[s].astype(jnp.float32)
        tile = jnp.where(s < count_ref[0], tile, 0.0)
        tile_ref[s] = tile.astype(jnp.bfloat16)
        turned_ref[s] = tile.T.astype(jnp.bfloat16)
        return 0

    def far(s, _):
        row = lax.broadcasted_iota(jnp.int32, left_ref.shape[1:], 0)
        left = jnp.where(row < rank_ref[s], left_ref[s].astype(jnp.float32), 0.0)
        right = right_ref[s]
        left = left.astype(jnp.bfloat16)
        tile = contract(left, right, ((0,), (0,)))
        tile_ref[near_slots + s] = tile.astype(jnp.bfloat16)
        turned_ref[near_slots + s] = tile.T.astype(jnp.bfloat16)
        return 0

    lax.fori_loop(0, near_slots, near, 0, unroll=4)
    lax.fori_loop(0, far_slots, far, 0, unroll=4)


def tile_sums(from_ref, to_ref, tile_ref, cells, total):
    total[...] = jnp.zeros_like(total)

    def step(s, _):
        product = contract(cells[from_ref[s]], tile_ref[s], ((1,), (0,)))
        total[to_ref[s]] = total[to_ref[s]] + product
        return 0

    lax.fori_loop(0, tile_ref.shape[0], step, 0, unroll=8)


def place(block, ref, cells):
    leaf = cells.shape[-1]
    per = ref.shape[-1] // leaf
    for j in range(per):
        cells[block * per + j] = ref[:, j * leaf : (j + 1) * leaf]


def rows_kernel(place_ref, from_ref, to_ref, tile_ref, *refs):
    blocks, (send_ref, keep_ref, cells, total) = refs[:-4], refs[-4:]
    leaf = cells.shape[-1]
    me, core = place_ref[0], place_ref[1] % 2
    for flip, ref in enumerate(blocks):
        place(me ^ flip, ref, cells)
    tile_sums(from_ref, to_ref, tile_ref, cells, total)
    chips, _, width = send_ref.shape
    per = width // leaf
    for z in range(chips):
        for j in range(per):
            part = slice(j * leaf, (j + 1) * leaf)
            send_ref[z, :, part] = total[(2 * z + 1 - core) * per + j].astype(jnp.bfloat16)
            keep_ref[z, :, part] = total[(2 * z + core) * per + j]


def cols_kernel(place_ref, from_ref, to_ref, tile_ref, *refs):
    chips = lax.axis_size("col") // 2
    count = 2 * chips
    blocks, rest = refs[:count], refs[count:]
    outs, (cells, total) = rest[:-2], rest[-2:]
    leaf = cells.shape[-1]
    me = place_ref[1]
    for flip, ref in enumerate(blocks):
        place(me ^ flip, ref, cells)
    tile_sums(from_ref, to_ref, tile_ref, cells, total)
    per = outs[0].shape[-1] // leaf
    for flip, out in enumerate(outs):
        for j in range(per):
            part = total[(place_ref[0] ^ flip) * per + j]
            out[:, j * leaf : (j + 1) * leaf] = part.astype(out.dtype)


def pair_kernel(place_ref, keep_ref, got_ref, *outs):
    chip = place_ref[1] // 2
    for flip, out in enumerate(outs):
        z = chip ^ flip
        out[...] = (keep_ref[z] + got_ref[z].astype(jnp.float32)).astype(out.dtype)


def solve_kernel(matrix_ref, rhs_ref, out_ref):
    size = matrix_ref.shape[0]
    work = jnp.concatenate([matrix_ref[...], rhs_ref[...]], axis=1)
    row = lax.broadcasted_iota(jnp.int32, work.shape, 0)
    for k in range(size):
        pivot_row = work[k : k + 1, :] / work[k : k + 1, k : k + 1]
        work = jnp.where(row == k, pivot_row, work - work[:, k : k + 1] * pivot_row)
    out_ref[...] = work[:, size:]


def small_solve(matrix, rhs):
    return pl.pallas_call(
        solve_kernel,
        out_shape=f32(*rhs.shape),
        in_specs=[vmem, vmem],
        out_specs=vmem,
        compiler_params=params,
        name="small_solve",
    )(matrix, rhs)


def inner(left_rows, right_rows):
    return jnp.dot(
        left_rows, right_rows.T, preferred_element_type=jnp.float32, precision=HIGHEST
    )


def combine(weights, rows_in):
    return jnp.dot(weights.T, rows_in, preferred_element_type=jnp.float32, precision=HIGHEST)


def sum_all(value):
    value = value + partner_permute(value, "col", 1)
    parts = [partner_permute(value, "col", 2 * k) for k in range(1, lax.axis_size("col") // 2)]
    value = functools.reduce(jnp.add, parts, value)
    parts = [partner_permute(value, "row", k) for k in range(1, lax.axis_size("row"))]
    return functools.reduce(jnp.add, parts, value)


def local(
    right_side,
    self_term,
    near_tiles,
    near_rows,
    near_cols,
    near_count,
    far_left,
    far_right,
    far_rows,
    far_cols,
    far_rank,
):
    cases, width = right_side.shape
    leaf = near_tiles.shape[-1]
    per = width // leaf
    rows, cols = lax.axis_size("row"), lax.axis_size("col")
    chips = cols // 2
    slots = near_tiles.shape[2] + far_left.shape[2]
    here = jnp.stack([lax.axis_index("row"), lax.axis_index("col")]).astype(jnp.int32)
    list_p = jnp.concatenate([near_rows[0, 0], far_rows[0, 0]])
    list_q = jnp.concatenate([near_cols[0, 0], far_cols[0, 0]])
    tiles, turned = pl.pallas_call(
        dense_kernel,
        out_shape=[bf16(slots, leaf, leaf)] * 2,
        in_specs=[smem, smem, vmem, vmem, vmem],
        out_specs=[vmem, vmem],
        compiler_params=params,
        name="dense_tiles",
    )(near_count[0], far_rank[0, 0], near_tiles[0, 0], far_left[0, 0], far_right[0, 0])

    def off_diagonal(vector):
        over_row = [partner_permute(vector, "row", k) for k in range(1, rows)]
        over_chip = [partner_permute(vector, "col", 2 * k) for k in range(1, chips)]
        other_core = [partner_permute(v, "col", 1) for v in [vector] + over_chip]
        send, keep = pl.pallas_call(
            rows_kernel,
            out_shape=[bf16(chips, cases, width), f32(chips, cases, width)],
            in_specs=[smem, smem, smem] + [vmem] * (1 + rows),
            out_specs=[vmem, vmem],
            scratch_shapes=[
                pltpu.VMEM((rows * per, cases, leaf), jnp.bfloat16),
                pltpu.VMEM((cols * per, cases, leaf), jnp.float32),
            ],
            compiler_params=params,
            cost_estimate=pl.CostEstimate(
                flops=2 * slots * cases * leaf * leaf * 8, bytes_accessed=0, transcendentals=0
            ),
            name="rows_half",
        )(here, list_q, list_p, turned, vector, *over_row)
        got = partner_permute(send, "col", 1)
        row_group = [None] * cols
        for k, (a, b) in enumerate(zip([vector] + over_chip, other_core)):
            row_group[2 * k], row_group[2 * k + 1] = a, b
        col_outs = pl.pallas_call(
            cols_kernel,
            out_shape=[f32(cases, width)] + [bf16(cases, width)] * (rows - 1),
            in_specs=[smem, smem, smem] + [vmem] * (1 + cols),
            out_specs=[vmem] * rows,
            scratch_shapes=[
                pltpu.VMEM((cols * per, cases, leaf), jnp.bfloat16),
                pltpu.VMEM((rows * per, cases, leaf), jnp.float32),
            ],
            compiler_params=params,
            cost_estimate=pl.CostEstimate(
                flops=2 * slots * cases * leaf * leaf * 8, bytes_accessed=0, transcendentals=0
            ),
            name="cols_half",
        )(here, list_p, list_q, tiles, *row_group)
        pair_outs = pl.pallas_call(
            pair_kernel,
            out_shape=[f32(cases, width)] + [bf16(cases, width)] * (chips - 1),
            in_specs=[smem, vmem, vmem],
            out_specs=[vmem] * chips,
            compiler_params=params,
            name="pair_sums",
        )(here, keep, got)
        arrived = [partner_permute(m, "col", 2 * k) for k, m in enumerate(pair_outs) if k]
        arrived += [partner_permute(m, "row", k) for k, m in enumerate(col_outs) if k]
        total = pair_outs[0] + col_outs[0]
        for message in arrived:
            total = total + message.astype(jnp.float32)
        return total

    diagonal = self_term[None, :]
    b = right_side
    w0 = diagonal * b + off_diagonal(b.astype(jnp.bfloat16))
    u0 = w0 - SHIFT * b
    gram = sum_all(jnp.concatenate([inner(b, b), inner(b, w0)], axis=1))
    rr0, curvature0 = gram[:, :cases], gram[:, cases:]
    aw0 = diagonal * u0 + off_diagonal(u0.astype(jnp.bfloat16)) + SHIFT * w0
    alpha0 = small_solve(curvature0, rr0)
    x1 = combine(alpha0, b)
    r1 = b - combine(alpha0, w0)
    w1 = w0 - combine(alpha0, aw0)
    u1 = w1 - SHIFT * r1
    gram = sum_all(jnp.concatenate([inner(r1, r1), inner(r1, w1)], axis=1))
    rr1, r1w1 = gram[:, :cases], gram[:, cases:]
    aw1 = diagonal * u1 + off_diagonal(u1.astype(jnp.bfloat16)) + SHIFT * w1
    beta0 = small_solve(rr0, rr1)
    curvature1 = r1w1 - combine(beta0, jnp.dot(curvature0, beta0, precision=HIGHEST))
    alpha1 = small_solve(curvature1, rr1)
    d1 = r1 + combine(beta0, b)
    s1 = w1 + combine(beta0, w0)
    x2 = x1 + combine(alpha1, d1)
    r2 = r1 - combine(alpha1, s1)
    w2 = w1 - combine(alpha1, aw1 + combine(beta0, aw0))
    gram = sum_all(jnp.concatenate([inner(r2, r2), inner(r2, w2)], axis=1))
    rr2, r2w2 = gram[:, :cases], gram[:, cases:]
    beta1 = small_solve(rr1, rr2)
    curvature2 = r2w2 - combine(beta1, jnp.dot(curvature1, beta1, precision=HIGHEST))
    alpha2 = small_solve(curvature2, rr2)
    d2 = r2 + combine(beta1, d1)
    s2 = w2 + combine(beta1, s1)
    return (x2 + combine(alpha2, d2), r2 - combine(alpha2, s2))


def solution(mesh):
    in_specs = (
        P(None, ("row", "col")),
        P(("row", "col")),
        P("row", "col", None, None, None),
        P("row", "col", None),
        P("row", "col", None),
        P("row", "col"),
        P("row", "col", None, None, None),
        P("row", "col", None, None, None),
        P("row", "col", None),
        P("row", "col", None),
        P("row", "col", None),
    )
    out_specs = (P(None, ("row", "col")), P(None, ("row", "col")))
    return jax.shard_map(local, mesh=mesh, in_specs=in_specs, out_specs=out_specs, check_vma=False)
```

```python
import functools

import jax
import jax.numpy as jnp
from jax import lax
from jax.experimental import pallas as pl
from jax.experimental.pallas import tpu as pltpu
from jax.sharding import PartitionSpec as P

VMEM_BYTES = 48 * 1024 * 1024
HIGHEST = lax.Precision.HIGHEST
GRAM = 128
PIECES = 3

vmem = pl.BlockSpec(memory_space=pltpu.VMEM)
smem = pl.BlockSpec(memory_space=pltpu.SMEM)
params = pltpu.CompilerParams(vmem_limit_bytes=VMEM_BYTES)


def f32(*shape):
    return jax.ShapeDtypeStruct(shape, jnp.float32)


def bf16(*shape):
    return jax.ShapeDtypeStruct(shape, jnp.bfloat16)


def contract(left, right, dims, precision=None):
    return lax.dot_general(
        left, right, (dims, ((), ())), precision=precision, preferred_element_type=jnp.float32
    )


def mul(left, right):
    return contract(left, right, ((1,), (0,)), HIGHEST)


def mul_t(left, right):
    return contract(left, right, ((0,), (0,)), HIGHEST)


def symmetric(matrix):
    return 0.5 * (matrix + matrix.T)


def partner_permute(value, axis, flip):
    size = lax.axis_size(axis)
    return lax.ppermute(value, axis, [(i, i ^ flip) for i in range(size)])


def put_gram(ref, width, gram):
    columns = gram.shape[1]
    for k in range(PIECES):
        piece = gram.astype(jnp.bfloat16)
        ref[:, width + k * columns : width + (k + 1) * columns] = piece
        gram = gram - piece.astype(jnp.float32)


def get_gram(ref, width):
    columns = (ref.shape[1] - width) // PIECES
    parts = [
        ref[:, width + k * columns : width + (k + 1) * columns].astype(jnp.float32)
        for k in range(PIECES)
    ]
    return (parts[2] + parts[1]) + parts[0]


def dense_kernel(count_ref, rank_ref, near_ref, left_ref, right_ref, tile_ref, turned_ref):
    near_slots, far_slots = near_ref.shape[0], left_ref.shape[0]

    def far(s, _):
        row = lax.broadcasted_iota(jnp.int32, left_ref.shape[1:], 0)
        left = jnp.where(row < rank_ref[s], left_ref[s].astype(jnp.float32), 0.0)
        left, right = left.astype(jnp.bfloat16), right_ref[s]
        tile_ref[near_slots + s] = contract(left, right, ((0,), (0,))).astype(jnp.bfloat16)
        turned_ref[near_slots + s] = contract(right, left, ((0,), (0,))).astype(jnp.bfloat16)
        return 0

    def near(s, _):
        tile = near_ref[s]
        tile = jnp.where(s < count_ref[0], tile, jnp.zeros_like(tile))
        tile_ref[s] = tile
        turned_ref[s] = tile.T
        return 0

    lax.fori_loop(0, far_slots, far, 0, unroll=8)
    lax.fori_loop(0, near_slots, near, 0, unroll=8)


def tile_sums(from_ref, to_ref, tile_ref, cells, total):
    total[...] = jnp.zeros_like(total)

    def step(s, _):
        product = contract(cells[from_ref[s]], tile_ref[s], ((1,), (0,)))
        total[to_ref[s]] = total[to_ref[s]] + product
        return 0

    lax.fori_loop(0, tile_ref.shape[0], step, 0, unroll=16)


def place(block, ref, cells, per):
    leaf = cells.shape[-1]
    for j in range(per):
        cells[block * per + j] = ref[:, j * leaf : (j + 1) * leaf]


def rows_kernel(place_ref, from_ref, to_ref, tile_ref, *refs):
    blocks, (send_ref, keep_ref, cells, total) = refs[:-4], refs[-4:]
    chips, _, width = send_ref.shape
    leaf = cells.shape[-1]
    per = width // leaf
    me, core = place_ref[0], place_ref[1] % 2
    for flip, ref in enumerate(blocks):
        place(me ^ flip, ref, cells, per)
    tile_sums(from_ref, to_ref, tile_ref, cells, total)
    for z in range(chips):
        for j in range(per):
            part = slice(j * leaf, (j + 1) * leaf)
            send_ref[z, :, part] = total[(2 * z + 1 - core) * per + j].astype(jnp.bfloat16)
            keep_ref[z, :, part] = total[(2 * z + core) * per + j]


def cols_kernel(rows, cols, place_ref, from_ref, to_ref, tile_ref, *refs):
    blocks, refs = refs[:cols], refs[cols:]
    outs, (cells, total) = refs[-rows - 3 : -2], refs[-2:]
    last = refs[: -rows - 3]
    own_ref, gram_ref, messages = outs[0], outs[1], outs[2:]
    width = own_ref.shape[1]
    leaf = cells.shape[-1]
    per = width // leaf
    me = place_ref[0]
    for flip, ref in enumerate(blocks):
        place(place_ref[1] ^ flip, ref, cells, per)
    tile_sums(from_ref, to_ref, tile_ref, cells, total)
    gram = get_gram(blocks[0], width)
    for ref in blocks[1:]:
        gram = gram + get_gram(ref, width)
    if last:
        vector_ref, diagonal_ref = last[rows:]
        vector = vector_ref[...]
        both = contract(vector, vector * diagonal_ref[...], ((1,), (1,)), HIGHEST)
        half = jnp.zeros_like(both)
        for flip, ref in enumerate(last[:rows]):
            for j in range(per):
                cluster = ref[:, j * leaf : (j + 1) * leaf]
                image = total[(me ^ flip) * per + j].astype(jnp.bfloat16)
                half = half + contract(cluster, image, ((1,), (1,)))
        both = both + 2.0 * half
        gram = jnp.concatenate([gram, both, jnp.zeros_like(both)], axis=1)
    gram_ref[...] = gram
    for flip, out in enumerate((own_ref, *messages)):
        for j in range(per):
            part = total[(me ^ flip) * per + j]
            out[:, j * leaf : (j + 1) * leaf] = part.astype(out.dtype)
    for out in messages:
        put_gram(out, width, gram)


def pair_kernel(place_ref, keep_ref, got_ref, *outs):
    chip = place_ref[1] // 2
    for flip, out in enumerate(outs):
        z = chip ^ flip
        out[...] = (keep_ref[z] + got_ref[z].astype(jnp.float32)).astype(out.dtype)


def first_kernel(vector_ref, diagonal_ref, message_ref):
    vector = vector_ref[...]
    width = vector.shape[1]
    message_ref[:, :width] = vector.astype(jnp.bfloat16)
    gram = contract(vector, vector, ((1,), (1,)), HIGHEST)
    weighted = jnp.sum(vector * vector * diagonal_ref[...], axis=1, keepdims=True)
    put_gram(
        message_ref, width, jnp.concatenate([gram, jnp.broadcast_to(weighted, gram.shape)], axis=1)
    )


def off_diagonal(rows, refs):
    width = refs[0].shape[1]
    total = refs[0][...] + refs[1][...]
    for ref in refs[2:]:
        total = total + ref[:, :width].astype(jnp.float32)
    return total


def sum_grams(own_ref, refs, width):
    gram = own_ref[...]
    for ref in refs:
        gram = gram + get_gram(ref, width)
    return gram


def combine_kernel(rows, first, vector_ref, diagonal_ref, shift_ref, gram_ref, *refs):
    sums, (next_ref, message_ref, total_ref) = refs[:-3], refs[-3:]
    width = vector_ref.shape[1]
    vector = vector_ref[...]
    gram = sum_grams(gram_ref, sums[1 - rows :], width)
    if first:
        cases = gram.shape[0]
        row = lax.broadcasted_iota(jnp.int32, (cases, cases), 0)
        column = lax.broadcasted_iota(jnp.int32, (cases, cases), 1)
        norm = jnp.sum(jnp.where(row == column, gram[:, :cases], 0.0), keepdims=True)
        shift = jnp.sum(gram[:, cases : cases + 1], keepdims=True) / norm
    else:
        shift = shift_ref[0:1, 0:1]
    total_ref[...] = gram
    following = (diagonal_ref[...] - shift) * vector + off_diagonal(rows, sums)
    next_ref[...] = following
    message_ref[:, :width] = following.astype(jnp.bfloat16)
    cross = contract(vector, following, ((1,), (1,)), HIGHEST)
    square = contract(following, following, ((1,), (1,)), HIGHEST)
    put_gram(message_ref, width, jnp.concatenate([cross, square], axis=1))


def shift_kernel(gram_ref, shift_ref):
    gram = gram_ref[...]
    cases = gram.shape[0]
    row = lax.broadcasted_iota(jnp.int32, (cases, cases), 0)
    column = lax.broadcasted_iota(jnp.int32, (cases, cases), 1)
    norm = jnp.sum(jnp.where(row == column, gram[:, :cases], 0.0), keepdims=True)
    shift = jnp.sum(gram[:, cases : cases + 1], keepdims=True) / norm
    shift_ref[...] = jnp.broadcast_to(shift, shift_ref.shape)


def last_gram_kernel(gram_ref, *refs):
    messages, (total_ref, both_ref) = refs[:-2], refs[-2:]
    width = messages[0].shape[1] - PIECES * gram_ref.shape[1]
    gram = sum_grams(gram_ref, messages, width)
    total_ref[...] = gram[:, :GRAM]
    both_ref[...] = gram[:, GRAM:]


def solve(*pairs):
    size = pairs[0][0].shape[0]
    works = [jnp.concatenate(pair, axis=1) for pair in pairs]
    row = lax.broadcasted_iota(jnp.int32, works[0].shape, 0)
    for k in range(size):
        pivots = [work[k : k + 1, :] / work[k : k + 1, k : k + 1] for work in works]
        works = [
            jnp.where(row == k, pivot, work - work[:, k : k + 1] * pivot)
            for work, pivot in zip(works, pivots)
        ]
    return [work[:, size:] for work in works]


def identity(size):
    row = lax.broadcasted_iota(jnp.int32, (size, size), 0)
    column = lax.broadcasted_iota(jnp.int32, (size, size), 1)
    return jnp.where(row == column, 1.0, 0.0)


def first_coefficients_kernel(shift_ref, gram0_ref, gram1_ref, out_ref):
    cases = gram0_ref.shape[0]
    shift = shift_ref[0:1, 0:1]
    bb = gram0_ref[:, :cases]
    bu, uu = gram1_ref[:, :cases], gram1_ref[:, cases:]
    one = identity(cases)
    alpha0, inverse = solve((shift * bb + symmetric(bu), bb), (bb, one))
    r_b = one - shift * alpha0
    r = jnp.concatenate([r_b, -alpha0], axis=0)
    gram = jnp.concatenate(
        [jnp.concatenate([bb, bu], axis=1), jnp.concatenate([bu.T, uu], axis=1)], axis=0
    )
    rr1 = symmetric(mul_t(r, mul(gram, r)))
    d_b = r_b + mul(inverse, rr1)
    out_ref[...] = jnp.concatenate([alpha0, rr1, r_b, d_b], axis=1)


def second_coefficients_kernel(
    shift_ref, gram0_ref, gram1_ref, gram2_ref, first_ref, vectors_ref, small_ref
):
    cases = gram0_ref.shape[0]
    shift = shift_ref[0:1, 0:1]
    bb = gram0_ref[:, :cases]
    bu, uu = gram1_ref[:, :cases], gram1_ref[:, cases:]
    uv, vv = gram2_ref[:, :cases], gram2_ref[:, cases:]
    bv = uu
    alpha0, rr1, r_b, d_b = [first_ref[:, k * cases : (k + 1) * cases] for k in range(4)]
    zero = jnp.zeros_like(bb)
    stack = functools.partial(jnp.concatenate, axis=0)
    side = functools.partial(jnp.concatenate, axis=1)
    gram = stack([side([bb, bu, bv]), side([bu.T, uu, uv]), side([bv, uv.T, vv])])
    r1 = stack([r_b, -alpha0, zero])
    d1 = stack([d_b, -alpha0, zero])
    s1 = stack([shift * d_b, d_b - shift * alpha0, -alpha0])
    curvature1 = symmetric(mul_t(d1, mul(gram, s1)))
    alpha1, inverse = solve((curvature1, rr1), (rr1, identity(cases)))
    r2 = r1 - mul(s1, alpha1)
    rr2 = symmetric(mul_t(r2, mul(gram, r2)))
    d2 = r2 + mul(d1, mul(inverse, rr2))
    d2_b, d2_u, d2_v = d2[:cases], d2[cases : 2 * cases], d2[2 * cases :]
    s2 = stack([shift * d2_b, d2_b + shift * d2_u, d2_u])
    with_y = mul_t(d2_b, uv + shift * bv) + mul_t(d2_u, vv + shift * uv)
    curvature2 = mul_t(d2, mul(gram, s2)) + mul(with_y, d2_v)
    x2 = stack([alpha0, zero, zero]) + mul(d1, alpha1)
    vectors_ref[...] = side([d2, r2, s2, x2])
    small_ref[...] = side([curvature2, rr2])


def finish_kernel(
    vectors_ref, small_ref, both_ref, other_ref, b_ref, u_ref, v_ref, diagonal_ref, *refs
):
    sums, (solution_ref, residual_ref) = refs[:-2], refs[-2:]
    cases = b_ref.shape[0]
    d2, r2, s2, x2 = [vectors_ref[:, k * cases : (k + 1) * cases] for k in range(4)]
    d2_v = d2[2 * cases :]
    both = symmetric(both_ref[:, :cases] + other_ref[:, :cases])
    curvature2 = symmetric(small_ref[:, :cases] + mul_t(d2_v, mul(both, d2_v)))
    (alpha2,) = solve((curvature2, small_ref[:, cases:]))
    y = diagonal_ref[...] * v_ref[...] + off_diagonal(0, sums)
    basis = jnp.concatenate([b_ref[...], u_ref[...], v_ref[...]], axis=0)
    solution_ref[...] = mul_t(x2 + mul(d2, alpha2), basis)
    residual_ref[...] = mul_t(r2 - mul(s2, alpha2), basis) - mul_t(mul(d2_v, alpha2), y)


def call(kernel, name, outs, *args, scratch=(), scalars=(), flops=0):
    scalars = set(scalars)
    return pl.pallas_call(
        kernel,
        out_shape=outs,
        in_specs=[smem if k in scalars else vmem for k in range(len(args))],
        out_specs=jax.tree.map(lambda _: vmem, outs),
        scratch_shapes=list(scratch),
        compiler_params=params,
        cost_estimate=pl.CostEstimate(flops=flops, bytes_accessed=0, transcendentals=0),
        name=name,
    )(*args)


def local(
    right_side,
    self_term,
    near_tiles,
    near_rows,
    near_cols,
    near_count,
    far_left,
    far_right,
    far_rows,
    far_cols,
    far_rank,
):
    cases, width = right_side.shape
    leaf = near_tiles.shape[-1]
    per = width // leaf
    rows, cols = lax.axis_size("row"), lax.axis_size("col")
    chips = cols // 2
    slots = near_tiles.shape[2] + far_left.shape[2]
    long = width + PIECES * GRAM
    here = jnp.stack([lax.axis_index("row"), lax.axis_index("col")]).astype(jnp.int32)
    list_p = jnp.concatenate([near_rows[0, 0], far_rows[0, 0]])
    list_q = jnp.concatenate([near_cols[0, 0], far_cols[0, 0]])
    diagonal = self_term[None, :]
    tiles, turned = call(
        dense_kernel,
        "dense_tiles",
        [bf16(slots, leaf, leaf)] * 2,
        near_count[0],
        far_rank[0, 0],
        near_tiles[0, 0],
        far_left[0, 0],
        far_right[0, 0],
        scalars=(0, 1),
    )
    half_flops = 2 * slots * cases * leaf * leaf * 8

    def apply(message, last=()):
        over_row = [partner_permute(message, "row", k) for k in range(1, rows)]
        over_chip = [partner_permute(message, "col", 2 * k) for k in range(1, chips)]
        other_core = [partner_permute(v, "col", 1) for v in [message] + over_chip]
        send, keep = call(
            rows_kernel,
            "rows_half",
            [bf16(chips, cases, width), f32(chips, cases, width)],
            here,
            list_q,
            list_p,
            turned,
            message,
            *over_row,
            scalars=(0, 1, 2),
            scratch=[
                pltpu.VMEM((rows * per, cases, leaf), jnp.bfloat16),
                pltpu.VMEM((cols * per, cases, leaf), jnp.float32),
            ],
            flops=half_flops,
        )
        got = partner_permute(send, "col", 1)
        row_group = [None] * cols
        for k, (a, b) in enumerate(zip([message] + over_chip, other_core)):
            row_group[2 * k], row_group[2 * k + 1] = a, b
        wide = 2 * GRAM if last else GRAM
        extra = [message, *over_row, *last] if last else []
        own_col, gram, *col_messages = call(
            functools.partial(cols_kernel, rows, cols),
            "cols_half",
            [f32(cases, width), f32(cases, wide)]
            + [bf16(cases, width + PIECES * wide)] * (rows - 1),
            here,
            list_p,
            list_q,
            tiles,
            *row_group,
            *extra,
            scalars=(0, 1, 2),
            scratch=[
                pltpu.VMEM((cols * per, cases, leaf), jnp.bfloat16),
                pltpu.VMEM((rows * per, cases, leaf), jnp.float32),
            ],
            flops=half_flops,
        )
        own_row, *row_messages = call(
            pair_kernel,
            "pair_sums",
            [f32(cases, width)] + [bf16(cases, width)] * (chips - 1),
            here,
            keep,
            got,
            scalars=(0,),
        )
        from_chips = [partner_permute(m, "col", 2 * k) for k, m in enumerate(row_messages, 1)]
        from_rows = [partner_permute(m, "row", k) for k, m in enumerate(col_messages, 1)]
        return [own_row, own_col, *from_chips], from_rows, gram

    def advance(first, vector, shift, parts):
        sums, from_rows, gram = parts
        return call(
            functools.partial(combine_kernel, rows, first),
            "combine",
            [f32(cases, width), bf16(cases, long), f32(cases, GRAM)],
            vector,
            diagonal,
            shift,
            gram,
            *sums,
            *from_rows,
        )

    b = right_side
    message = call(first_kernel, "first_message", bf16(cases, long), b, diagonal)
    u, message, gram0 = advance(True, b, diagonal, apply(message))
    shift = call(shift_kernel, "shift", f32(8, 128), gram0)
    v, message, gram1 = advance(False, u, shift, apply(message))
    first = call(
        first_coefficients_kernel, "coefficients", f32(cases, 4 * cases), shift, gram0, gram1
    )
    sums, from_rows, gram = apply(message, last=(v, diagonal))
    gram2, both = call(
        last_gram_kernel, "last_gram", [f32(cases, GRAM), f32(cases, GRAM)], gram, *from_rows
    )
    over_chip = [partner_permute(both, "col", 2 * k) for k in range(1, chips)]
    both = functools.reduce(jnp.add, over_chip, both)
    other = partner_permute(both, "col", 1)
    vectors, small = call(
        second_coefficients_kernel,
        "coefficients",
        [f32(3 * cases, 4 * cases), f32(cases, 2 * cases)],
        shift,
        gram0,
        gram1,
        gram2,
        first,
    )
    return call(
        finish_kernel,
        "finish",
        [f32(cases, width), f32(cases, width)],
        vectors,
        small,
        both,
        other,
        b,
        u,
        v,
        diagonal,
        *sums,
        *from_rows,
    )


def solution(mesh):
    in_specs = (
        P(None, ("row", "col")),
        P(("row", "col")),
        P("row", "col", None, None, None),
        P("row", "col", None),
        P("row", "col", None),
        P("row", "col"),
        P("row", "col", None, None, None),
        P("row", "col", None, None, None),
        P("row", "col", None),
        P("row", "col", None),
        P("row", "col", None),
    )
    out_specs = (P(None, ("row", "col")), P(None, ("row", "col")))
    return jax.shard_map(local, mesh=mesh, in_specs=in_specs, out_specs=out_specs, check_vma=False)
```

```python
import functools

import jax
import jax.numpy as jnp
from jax import lax
from jax.experimental import pallas as pl
from jax.experimental.pallas import tpu as pltpu
from jax.sharding import PartitionSpec as P

VMEM_BYTES = 24 * 1024 * 1024
DENSE_BYTES = 24 * 1024 * 1024
HIGHEST = lax.Precision.HIGHEST
GRAM = 128
PIECES = 2
PANEL = 8
UNROLL = 32

vmem = pl.BlockSpec(memory_space=pltpu.VMEM)
smem = pl.BlockSpec(memory_space=pltpu.SMEM)
hbm = pl.BlockSpec(memory_space=pltpu.HBM)


def f32(*shape):
    return jax.ShapeDtypeStruct(shape, jnp.float32)


def bf16(*shape):
    return jax.ShapeDtypeStruct(shape, jnp.bfloat16)


def contract(left, right, dims, precision=None):
    return lax.dot_general(
        left, right, (dims, ((), ())), precision=precision, preferred_element_type=jnp.float32
    )


def mul(left, right):
    return contract(left, right, ((1,), (0,)), HIGHEST)


def mul_t(left, right):
    return contract(left, right, ((0,), (0,)), HIGHEST)


def symmetric(matrix):
    return 0.5 * (matrix + matrix.T)


def partner_permute(value, axis, flip):
    size = lax.axis_size(axis)
    return lax.ppermute(value, axis, [(i, i ^ flip) for i in range(size)])


def put_gram(ref, width, gram):
    columns = gram.shape[1]
    for k in range(PIECES):
        piece = gram.astype(jnp.bfloat16)
        ref[:, width + k * columns : width + (k + 1) * columns] = piece
        gram = gram - piece.astype(jnp.float32)


def get_gram(ref, width):
    columns = (ref.shape[1] - width) // PIECES
    parts = [
        ref[:, width + k * columns : width + (k + 1) * columns].astype(jnp.float32)
        for k in range(PIECES)
    ]
    return functools.reduce(jnp.add, reversed(parts))


def dense_kernel(
    table, near_ref, left_ref, right_ref, tile_ref, turned_ref, lefts, rights, sems
):
    near_slots, far_slots = near_ref.shape[0], left_ref.shape[0]
    ranks = 2 + 2 * (near_slots + far_slots)
    count = table[ranks + far_slots]
    copies = [
        pltpu.make_async_copy(source, target, sems.at[k])
        for k, (source, target) in enumerate(
            [
                (left_ref, lefts),
                (right_ref, rights),
                (near_ref, tile_ref.at[pl.ds(0, near_slots)]),
            ]
        )
    ]
    for copy in copies:
        copy.start()
    copies[0].wait()
    copies[1].wait()

    def far(s, _):
        row = lax.broadcasted_iota(jnp.int32, lefts.shape[1:], 0)
        left = jnp.where(row < table[ranks + s], lefts[s].astype(jnp.float32), 0.0)
        left, right = left.astype(jnp.bfloat16), rights[s]
        tile_ref[near_slots + s] = contract(left, right, ((0,), (0,))).astype(jnp.bfloat16)
        turned_ref[near_slots + s] = contract(right, left, ((0,), (0,))).astype(jnp.bfloat16)
        return 0

    def near(s, _):
        tile = tile_ref[s]
        tile = jnp.where(s < count, tile, jnp.zeros_like(tile))
        tile_ref[s] = tile
        turned_ref[s] = tile.T
        return 0

    lax.fori_loop(0, far_slots, far, 0, unroll=16)
    copies[2].wait()
    lax.fori_loop(0, near_slots, near, 0, unroll=8)


def tile_sums(table, inputs, outputs, tile_ref, cells, total):
    total[...] = jnp.zeros_like(total)

    def step(s, _):
        product = contract(cells[table[inputs + s]], tile_ref[s], ((1,), (0,)))
        to = table[outputs + s]
        total[to] = total[to] + product
        return 0

    lax.fori_loop(0, tile_ref.shape[0], step, 0, unroll=UNROLL)


def place(block, ref, cells, per):
    leaf = cells.shape[-1]
    for j in range(per):
        cells[block * per + j] = ref[:, j * leaf : (j + 1) * leaf]


def rows_kernel(table, tile_ref, *refs):
    blocks, (send_ref, keep_ref, cells, total) = refs[:-4], refs[-4:]
    chips, _, width = send_ref.shape
    leaf = cells.shape[-1]
    per = width // leaf
    me, core = table[0], table[1] % 2
    for flip, ref in enumerate(blocks):
        place(me ^ flip, ref, cells, per)
    slots = tile_ref.shape[0]
    tile_sums(table, 2 + slots, 2, tile_ref, cells, total)
    for z in range(chips):
        for j in range(per):
            part = slice(j * leaf, (j + 1) * leaf)
            send_ref[z, :, part] = total[(2 * z + 1 - core) * per + j].astype(jnp.bfloat16)
            keep_ref[z, :, part] = total[(2 * z + core) * per + j]


def cols_kernel(rows, cols, table, tile_ref, *refs):
    blocks, refs = refs[:cols], refs[cols:]
    outs, (cells, total) = refs[-rows - 3 : -2], refs[-2:]
    last = refs[: -rows - 3]
    own_ref, gram_ref, messages = outs[0], outs[1], outs[2:]
    width = own_ref.shape[1]
    leaf = cells.shape[-1]
    per = width // leaf
    me = table[0]
    for flip, ref in enumerate(blocks):
        place(table[1] ^ flip, ref, cells, per)
    slots = tile_ref.shape[0]
    tile_sums(table, 2, 2 + slots, tile_ref, cells, total)
    gram = get_gram(blocks[0], width)
    for ref in blocks[1:]:
        gram = gram + get_gram(ref, width)
    if last:
        vector_ref, diagonal_ref = last[rows:]
        vector = vector_ref[...]
        both = contract(vector, vector * diagonal_ref[...], ((1,), (1,)), HIGHEST)
        half = jnp.zeros_like(both)
        for flip, ref in enumerate(last[:rows]):
            for j in range(per):
                cluster = ref[:, j * leaf : (j + 1) * leaf]
                image = total[(me ^ flip) * per + j].astype(jnp.bfloat16)
                half = half + contract(cluster, image, ((1,), (1,)))
        both = both + 2.0 * half
        gram = jnp.concatenate([gram, both], axis=1)
    gram_ref[...] = gram
    for flip, out in enumerate((own_ref, *messages)):
        for j in range(per):
            part = total[(me ^ flip) * per + j]
            out[:, j * leaf : (j + 1) * leaf] = part.astype(out.dtype)
    for out in messages:
        put_gram(out, width, gram)


def pair_kernel(table, keep_ref, got_ref, *outs):
    chip = table[1] // 2
    for flip, out in enumerate(outs):
        z = chip ^ flip
        out[...] = (keep_ref[z] + got_ref[z].astype(jnp.float32)).astype(out.dtype)


def chip_sums_kernel(own_ref, *refs):
    total = own_ref[...]
    for ref in refs[:-1]:
        total = total + ref[...].astype(jnp.float32)
    refs[-1][...] = total


def first_kernel(vector_ref, diagonal_ref, message_ref):
    vector = vector_ref[...]
    width = vector.shape[1]
    message_ref[:, :width] = vector.astype(jnp.bfloat16)
    gram = contract(vector, vector, ((1,), (1,)), HIGHEST)
    weighted = jnp.sum(vector * vector * diagonal_ref[...], axis=1, keepdims=True)
    put_gram(
        message_ref, width, jnp.concatenate([gram, jnp.broadcast_to(weighted, gram.shape)], axis=1)
    )


def off_diagonal(refs):
    width = refs[0].shape[1]
    total = refs[0][...] + refs[1][...]
    for ref in refs[2:]:
        total = total + ref[:, :width].astype(jnp.float32)
    return total


def sum_grams(own_ref, refs, width):
    gram = own_ref[...]
    for ref in refs:
        gram = gram + get_gram(ref, width)
    return gram


def combine_kernel(rows, first, vector_ref, diagonal_ref, shift_ref, gram_ref, *refs):
    sums, (next_ref, message_ref, total_ref) = refs[:-3], refs[-3:]
    width = vector_ref.shape[1]
    vector = vector_ref[...]
    gram = sum_grams(gram_ref, sums[1 - rows :], width)
    if first:
        cases = gram.shape[0]
        row = lax.broadcasted_iota(jnp.int32, (cases, cases), 0)
        column = lax.broadcasted_iota(jnp.int32, (cases, cases), 1)
        norm = jnp.sum(jnp.where(row == column, gram[:, :cases], 0.0), keepdims=True)
        shift = jnp.sum(gram[:, cases : cases + 1], keepdims=True) / norm
    else:
        shift = shift_ref[0:1, 0:1]
    total_ref[...] = gram
    following = (diagonal_ref[...] - shift) * vector + off_diagonal(sums)
    next_ref[...] = following
    message_ref[:, :width] = following.astype(jnp.bfloat16)
    cross = contract(vector, following, ((1,), (1,)), HIGHEST)
    square = contract(following, following, ((1,), (1,)), HIGHEST)
    put_gram(message_ref, width, jnp.concatenate([cross, square], axis=1))


def shift_kernel(gram_ref, shift_ref):
    gram = gram_ref[...]
    cases = gram.shape[0]
    row = lax.broadcasted_iota(jnp.int32, (cases, cases), 0)
    column = lax.broadcasted_iota(jnp.int32, (cases, cases), 1)
    norm = jnp.sum(jnp.where(row == column, gram[:, :cases], 0.0), keepdims=True)
    shift = jnp.sum(gram[:, cases : cases + 1], keepdims=True) / norm
    shift_ref[...] = jnp.broadcast_to(shift, shift_ref.shape)


def last_gram_kernel(gram_ref, *refs):
    messages, (total_ref, both_ref) = refs[:-2], refs[-2:]
    width = messages[0].shape[1] - PIECES * gram_ref.shape[1]
    gram = sum_grams(gram_ref, messages, width)
    total_ref[...] = gram[:, :GRAM]
    both_ref[...] = gram[:, GRAM:]


def solve(*pairs):
    size = pairs[0][0].shape[0]
    works = [jnp.concatenate(pair, axis=1) for pair in pairs]
    shape = works[0].shape
    row = lax.broadcasted_iota(jnp.int32, shape, 0)
    for start in range(0, size, PANEL):
        panel = range(start, start + PANEL)
        spread = [[jnp.broadcast_to(w[:, k : k + 1], shape) for k in panel] for w in works]
        for k in panel:
            for n, columns in enumerate(spread):
                pivot = columns[0]
                inverse = 1.0 / pivot[k : k + 1, :]

                def eliminate(matrix):
                    pivot_row = matrix[k : k + 1, :] * inverse
                    return jnp.where(row == k, pivot_row, matrix - pivot * pivot_row)

                works[n] = eliminate(works[n])
                spread[n] = [eliminate(column) for column in columns[1:]]
    return [work[:, size:] for work in works]


def identity(size):
    row = lax.broadcasted_iota(jnp.int32, (size, size), 0)
    column = lax.broadcasted_iota(jnp.int32, (size, size), 1)
    return jnp.where(row == column, 1.0, 0.0)


def first_coefficients_kernel(shift_ref, gram0_ref, gram1_ref, out_ref):
    cases = gram0_ref.shape[0]
    shift = shift_ref[0:1, 0:1]
    bb = gram0_ref[:, :cases]
    bu, uu = gram1_ref[:, :cases], gram1_ref[:, cases:]
    one = identity(cases)
    alpha0, inverse = solve((shift * bb + symmetric(bu), bb), (bb, one))
    r_b = one - shift * alpha0
    r = jnp.concatenate([r_b, -alpha0], axis=0)
    gram = jnp.concatenate(
        [jnp.concatenate([bb, bu], axis=1), jnp.concatenate([bu.T, uu], axis=1)], axis=0
    )
    rr1 = symmetric(mul_t(r, mul(gram, r)))
    d_b = r_b + mul(inverse, rr1)
    out_ref[...] = jnp.concatenate([alpha0, rr1, r_b, d_b], axis=1)


def second_coefficients_kernel(
    shift_ref, gram0_ref, gram1_ref, gram2_ref, first_ref, big_ref, small_ref
):
    cases = gram0_ref.shape[0]
    shift = shift_ref[0:1, 0:1]
    bb = gram0_ref[:, :cases]
    bu, uu = gram1_ref[:, :cases], gram1_ref[:, cases:]
    uv, vv = gram2_ref[:, :cases], gram2_ref[:, cases:]
    bv = uu
    alpha0, rr1, r_b, d_b = [first_ref[:, k * cases : (k + 1) * cases] for k in range(4)]
    zero = jnp.zeros_like(bb)
    stack = functools.partial(jnp.concatenate, axis=0)
    side = functools.partial(jnp.concatenate, axis=1)
    gram = stack([side([bb, bu, bv]), side([bu.T, uu, uv]), side([bv, uv.T, vv])])
    r1 = stack([r_b, -alpha0, zero])
    d1 = stack([d_b, -alpha0, zero])
    s1 = stack([shift * d_b, d_b - shift * alpha0, -alpha0])
    curvature1 = symmetric(mul_t(d1, mul(gram, s1)))
    alpha1, inverse = solve((curvature1, rr1), (rr1, identity(cases)))
    r2 = r1 - mul(s1, alpha1)
    rr2 = symmetric(mul_t(r2, mul(gram, r2)))
    d2 = r2 + mul(d1, mul(inverse, rr2))
    d2_b, d2_u, d2_v = d2[:cases], d2[cases : 2 * cases], d2[2 * cases :]
    s2 = stack([shift * d2_b, d2_b + shift * d2_u, d2_u])
    with_y = mul_t(d2_b, uv + shift * bv) + mul_t(d2_u, vv + shift * uv)
    curvature2 = mul_t(d2, mul(gram, s2)) + mul(with_y, d2_v)
    x2 = stack([alpha0, zero, zero]) + mul(d1, alpha1)
    small_ref[...] = side([curvature2, rr2, d2_v, zero])
    big_ref[...] = side([d2, r2, s2, x2])


def vectors_kernel(big_ref, b_ref, u_ref, v_ref, vectors_ref):
    basis = jnp.concatenate([b_ref[...], u_ref[...], v_ref[...]], axis=0)
    vectors_ref[...] = mul_t(big_ref[...], basis)


def finish_kernel(vectors_ref, small_ref, both_ref, other_ref, v_ref, diagonal_ref, *refs):
    sums, (solution_ref, residual_ref) = refs[:-2], refs[-2:]
    cases = v_ref.shape[0]
    d2, r2, s2, x2 = [vectors_ref[k * cases : (k + 1) * cases, :] for k in range(4)]
    curvature2, rr2, d2_v = [small_ref[:, k * cases : (k + 1) * cases] for k in range(3)]
    both = symmetric(both_ref[...] + other_ref[...])
    (alpha2,) = solve((symmetric(curvature2 + mul_t(d2_v, mul(both, d2_v))), rr2))
    y = diagonal_ref[...] * v_ref[...] + off_diagonal(sums)
    s2 = s2 + mul_t(d2_v, y)
    solution_ref[...] = x2 + mul_t(alpha2, d2)
    residual_ref[...] = r2 - mul_t(alpha2, s2)


def call(kernel, name, outs, *args, scratch=(), scalars=(), far=(), cost=0, room=VMEM_BYTES):
    spaces = {**dict.fromkeys(scalars, smem), **dict.fromkeys(far, hbm)}
    return pl.pallas_call(
        kernel,
        out_shape=outs,
        in_specs=[spaces.get(k, vmem) for k in range(len(args))],
        out_specs=jax.tree.map(lambda _: vmem, outs),
        scratch_shapes=list(scratch),
        compiler_params=pltpu.CompilerParams(vmem_limit_bytes=room),
        cost_estimate=pl.CostEstimate(flops=int(cost * 1e9), bytes_accessed=0, transcendentals=0),
        name=name,
    )(*args)


def local(
    right_side,
    self_term,
    near_tiles,
    near_rows,
    near_cols,
    near_count,
    far_left,
    far_right,
    far_rows,
    far_cols,
    far_rank,
):
    cases, width = right_side.shape
    leaf = near_tiles.shape[-1]
    per = width // leaf
    rows, cols = lax.axis_size("row"), lax.axis_size("col")
    chips = cols // 2
    slots = near_tiles.shape[2] + far_left.shape[2]
    long = width + PIECES * GRAM
    table = jnp.concatenate(
        [
            jnp.stack([lax.axis_index("row"), lax.axis_index("col")]).astype(jnp.int32),
            near_rows[0, 0],
            far_rows[0, 0],
            near_cols[0, 0],
            far_cols[0, 0],
            far_rank[0, 0],
            near_count[0],
        ]
    )
    diagonal = self_term[None, :]
    tiles, turned = call(
        dense_kernel,
        "dense_tiles",
        [bf16(slots, leaf, leaf)] * 2,
        table,
        near_tiles[0, 0],
        far_left[0, 0],
        far_right[0, 0],
        scalars=(0,),
        far=(1, 2, 3),
        room=DENSE_BYTES,
        scratch=[
            pltpu.VMEM(far_left.shape[2:], jnp.bfloat16),
            pltpu.VMEM(far_right.shape[2:], jnp.bfloat16),
            pltpu.SemaphoreType.DMA((3,)),
        ],
    )

    def apply(message, last=(), beside=()):
        over_row = [partner_permute(message, "row", k) for k in range(1, rows)]
        over_chip = [partner_permute(message, "col", 2 * k) for k in range(1, chips)]
        send, keep = call(
            rows_kernel,
            "rows_half",
            [bf16(chips, cases, width), f32(chips, cases, width)],
            table,
            turned,
            message,
            *over_row,
            scalars=(0,),
            scratch=[
                pltpu.VMEM((rows * per, cases, leaf), jnp.bfloat16),
                pltpu.VMEM((cols * per, cases, leaf), jnp.float32),
            ],
            cost=0,
        )
        over_chip, beside, send, keep = lax.optimization_barrier((over_chip, beside, send, keep))
        got = partner_permute(send, "col", 1)
        own_chip, *row_messages = call(
            pair_kernel,
            "pair_sums",
            [f32(cases, width)] + [bf16(cases, width)] * (chips - 1),
            table,
            keep,
            got,
            scalars=(0,),
        )
        from_chips = [partner_permute(m, "col", 2 * k) for k, m in enumerate(row_messages, 1)]
        other_core = [partner_permute(v, "col", 1) for v in [message] + over_chip]
        own_row = call(
            chip_sums_kernel, "chip_sums", f32(cases, width), own_chip, *from_chips, cost=1
        )
        row_group = [None] * cols
        for k, (a, b) in enumerate(zip([message] + over_chip, other_core)):
            row_group[2 * k], row_group[2 * k + 1] = a, b
        wide = GRAM + cases if last else GRAM
        extra = [message, *over_row, *last] if last else []
        own_col, gram, *col_messages = call(
            functools.partial(cols_kernel, rows, cols),
            "cols_half",
            [f32(cases, width), f32(cases, wide)]
            + [bf16(cases, width + PIECES * wide)] * (rows - 1),
            table,
            tiles,
            *row_group,
            *extra,
            scalars=(0,),
            scratch=[
                pltpu.VMEM((cols * per, cases, leaf), jnp.bfloat16),
                pltpu.VMEM((rows * per, cases, leaf), jnp.float32),
            ],
            cost=0,
        )
        from_rows = [partner_permute(m, "row", k) for k, m in enumerate(col_messages, 1)]
        if last:
            from_rows, _ = lax.optimization_barrier((from_rows, own_row))
        return [own_row, own_col, *from_rows], from_rows, gram, beside

    def advance(first, vector, shift, parts):
        sums, from_rows, gram, _ = parts
        return call(
            functools.partial(combine_kernel, rows, first),
            "combine",
            [f32(cases, width), bf16(cases, long), f32(cases, GRAM)],
            vector,
            diagonal,
            shift,
            gram,
            *sums,
        )

    b = right_side
    message = call(first_kernel, "first_message", bf16(cases, long), b, diagonal, cost=10)
    u, message, gram0 = advance(True, b, diagonal, apply(message))
    shift = call(shift_kernel, "shift", f32(8, 128), gram0)
    v, message, gram1 = advance(False, u, shift, apply(message))
    first = call(
        first_coefficients_kernel, "coefficients", f32(cases, 4 * cases), shift, gram0, gram1
    )
    sums, from_rows, gram, first = apply(message, last=(v, diagonal), beside=first)
    gram2, both = call(
        last_gram_kernel, "last_gram", [f32(cases, GRAM), f32(cases, cases)], gram, *from_rows
    )
    over_chip = [partner_permute(both, "col", 2 * k) for k in range(1, chips)]
    big, small = call(
        second_coefficients_kernel,
        "coefficients",
        [f32(3 * cases, 4 * cases), f32(cases, 4 * cases)],
        shift,
        gram0,
        gram1,
        gram2,
        first,
    )
    over_chip, big = lax.optimization_barrier((over_chip, big))
    both = functools.reduce(jnp.add, over_chip, both)
    other = partner_permute(both, "col", 1)
    big, _ = lax.optimization_barrier((big, both))
    vectors = call(vectors_kernel, "vectors", f32(4 * cases, width), big, b, u, v)
    other, vectors = lax.optimization_barrier((other, vectors))
    return call(
        finish_kernel,
        "finish",
        [f32(cases, width), f32(cases, width)],
        vectors,
        small,
        both,
        other,
        v,
        diagonal,
        *sums,
    )


def solution(mesh):
    in_specs = (
        P(None, ("row", "col")),
        P(("row", "col")),
        P("row", "col", None, None, None),
        P("row", "col", None),
        P("row", "col", None),
        P("row", "col"),
        P("row", "col", None, None, None),
        P("row", "col", None, None, None),
        P("row", "col", None),
        P("row", "col", None),
        P("row", "col", None),
    )
    out_specs = (P(None, ("row", "col")), P(None, ("row", "col")))
    return jax.shard_map(local, mesh=mesh, in_specs=in_specs, out_specs=out_specs, check_vma=False)
```

```python
import functools

import jax
import jax.numpy as jnp
from jax import lax
from jax.experimental import pallas as pl
from jax.experimental.pallas import tpu as pltpu
from jax.sharding import PartitionSpec as P

VMEM_BYTES = 24 * 1024 * 1024
DENSE_BYTES = 24 * 1024 * 1024
HIGHEST = lax.Precision.HIGHEST
GRAM = 128
PIECES = 2
UNROLL = 32

vmem = pl.BlockSpec(memory_space=pltpu.VMEM)
smem = pl.BlockSpec(memory_space=pltpu.SMEM)
hbm = pl.BlockSpec(memory_space=pltpu.HBM)


def f32(*shape):
    return jax.ShapeDtypeStruct(shape, jnp.float32)


def bf16(*shape):
    return jax.ShapeDtypeStruct(shape, jnp.bfloat16)


def contract(left, right, dims, precision=None):
    return lax.dot_general(
        left, right, (dims, ((), ())), precision=precision, preferred_element_type=jnp.float32
    )


def mul(left, right):
    return contract(left, right, ((1,), (0,)), HIGHEST)


def mul_t(left, right):
    return contract(left, right, ((0,), (0,)), HIGHEST)


def symmetric(matrix):
    return 0.5 * (matrix + matrix.T)


def partner_permute(value, axis, flip):
    size = lax.axis_size(axis)
    return lax.ppermute(value, axis, [(i, i ^ flip) for i in range(size)])


def put_gram(ref, first, gram):
    columns = gram.shape[1]
    for k in range(PIECES):
        piece = gram.astype(jnp.bfloat16)
        ref[:, first + k * columns : first + (k + 1) * columns] = piece
        gram = gram - piece.astype(jnp.float32)


def get_gram(ref, first, columns):
    parts = [
        ref[:, first + k * columns : first + (k + 1) * columns].astype(jnp.float32)
        for k in range(PIECES)
    ]
    return functools.reduce(jnp.add, reversed(parts))


def dense_kernel(
    table, near_ref, left_ref, right_ref, tile_ref, turned_ref, lefts, rights, sems
):
    near_slots, far_slots = near_ref.shape[0], left_ref.shape[0]
    ranks = 2 + 2 * (near_slots + far_slots)
    count = table[ranks + far_slots]
    copies = [
        pltpu.make_async_copy(source, target, sems.at[k])
        for k, (source, target) in enumerate(
            [
                (left_ref, lefts),
                (right_ref, rights),
                (near_ref, tile_ref.at[pl.ds(0, near_slots)]),
            ]
        )
    ]
    for copy in copies:
        copy.start()
    copies[0].wait()
    copies[1].wait()

    def far(s, _):
        row = lax.broadcasted_iota(jnp.int32, lefts.shape[1:], 0)
        left = jnp.where(row < table[ranks + s], lefts[s].astype(jnp.float32), 0.0)
        left, right = left.astype(jnp.bfloat16), rights[s]
        tile_ref[near_slots + s] = contract(left, right, ((0,), (0,))).astype(jnp.bfloat16)
        turned_ref[near_slots + s] = contract(right, left, ((0,), (0,))).astype(jnp.bfloat16)
        return 0

    def near(s, _):
        tile = tile_ref[s]
        tile = jnp.where(s < count, tile, jnp.zeros_like(tile))
        tile_ref[s] = tile
        turned_ref[s] = tile.T
        return 0

    lax.fori_loop(0, far_slots, far, 0, unroll=16)
    copies[2].wait()
    lax.fori_loop(0, near_slots, near, 0, unroll=8)


def tile_sums(table, inputs, outputs, tile_ref, cells, total):
    total[...] = jnp.zeros_like(total)

    def step(s, _):
        product = contract(cells[table[inputs + s]], tile_ref[s], ((1,), (0,)))
        to = table[outputs + s]
        total[to] = total[to] + product
        return 0

    lax.fori_loop(0, tile_ref.shape[0], step, 0, unroll=UNROLL)


def place(block, ref, cells, per):
    leaf = cells.shape[-1]
    for j in range(per):
        cells[block * per + j] = ref[:, j * leaf : (j + 1) * leaf]


def rows_kernel(table, tile_ref, *refs):
    blocks, (send_ref, keep_ref, gram_ref, cells, total) = refs[:-5], refs[-5:]
    chips, _, width = keep_ref.shape
    leaf = cells.shape[-1]
    per = width // leaf
    me, core = table[0], table[1] % 2
    for flip, ref in enumerate(blocks):
        place(me ^ flip, ref, cells, per)
    slots = tile_ref.shape[0]
    tile_sums(table, 2 + slots, 2, tile_ref, cells, total)
    for z in range(chips):
        for j in range(per):
            part = slice(j * leaf, (j + 1) * leaf)
            send_ref[z, :, part] = total[(2 * z + 1 - core) * per + j].astype(jnp.bfloat16)
            keep_ref[z, :, part] = total[(2 * z + core) * per + j]
    gram = functools.reduce(jnp.add, [get_gram(ref, width, GRAM) for ref in blocks])
    gram_ref[...] = gram
    send_ref[chips] = jnp.zeros(send_ref.shape[1:], send_ref.dtype)
    put_gram(send_ref.at[chips], 0, gram)


def cols_kernel(rows, cols, table, tile_ref, *refs):
    blocks, refs, (cells, total) = refs[:cols], refs[cols:-2], refs[-2:]
    last = refs[: rows + 2] if len(refs) > rows else ()
    outs = refs[len(last) : len(last) + rows]
    width = outs[0].shape[1]
    leaf = cells.shape[-1]
    per = width // leaf
    me = table[0]
    for flip, ref in enumerate(blocks):
        place(table[1] ^ flip, ref, cells, per)
    slots = tile_ref.shape[0]
    tile_sums(table, 2, 2 + slots, tile_ref, cells, total)
    for flip, out in enumerate(outs):
        for j in range(per):
            part = total[(me ^ flip) * per + j]
            out[:, j * leaf : (j + 1) * leaf] = part.astype(out.dtype)
    if last:
        vector_ref, diagonal_ref = last[rows:]
        vector = vector_ref[...]
        both = contract(vector, vector * diagonal_ref[...], ((1,), (1,)), HIGHEST)
        half = jnp.zeros_like(both)
        for flip, ref in enumerate(last[:rows]):
            for j in range(per):
                cluster = ref[:, j * leaf : (j + 1) * leaf]
                image = total[(me ^ flip) * per + j].astype(jnp.bfloat16)
                half = half + contract(cluster, image, ((1,), (1,)))
        both = both + 2.0 * half
        refs[-1][...] = both
        for out in outs[1:]:
            put_gram(out, width, both)


def pair_kernel(table, keep_ref, gram_ref, got_ref, own_ref, own_gram_ref, *messages):
    chips, _, width = keep_ref.shape
    chip = table[1] // 2
    gram = gram_ref[...] + get_gram(got_ref.at[chips], 0, GRAM)
    own_gram_ref[...] = gram
    for flip, out in enumerate((own_ref, *messages)):
        z = chip ^ flip
        out[:, :width] = (keep_ref[z] + got_ref[z].astype(jnp.float32)).astype(out.dtype)
    for out in messages:
        put_gram(out, width, gram)


def chip_sums_kernel(own_ref, gram_ref, *refs):
    messages, (out_ref, total_ref) = refs[:-2], refs[-2:]
    width = own_ref.shape[1]
    total, gram = own_ref[...], gram_ref[...]
    for ref in messages:
        total = total + ref[:, :width].astype(jnp.float32)
        gram = gram + get_gram(ref, width, GRAM)
    out_ref[...] = total
    total_ref[...] = gram


def put_vector(vector, gram, plain_ref, wide_ref):
    rounded = vector.astype(jnp.bfloat16)
    width = vector.shape[1]
    plain_ref[...] = rounded
    wide_ref[:, :width] = rounded
    put_gram(wide_ref, width, gram)


def first_kernel(vector_ref, diagonal_ref, plain_ref, wide_ref):
    vector = vector_ref[...]
    gram = contract(vector, vector, ((1,), (1,)), HIGHEST)
    weighted = jnp.sum(vector * vector * diagonal_ref[...], axis=1, keepdims=True)
    gram = jnp.concatenate([gram, jnp.broadcast_to(weighted, gram.shape)], axis=1)
    put_vector(vector, gram, plain_ref, wide_ref)


def off_diagonal(refs):
    width = refs[0].shape[1]
    total = refs[0][...] + refs[1][...]
    for ref in refs[2:]:
        total = total + ref[:, :width].astype(jnp.float32)
    return total


def rayleigh(gram):
    cases = gram.shape[0]
    norm = jnp.sum(identity(cases) * gram[:, :cases], keepdims=True)
    return jnp.sum(gram[:, cases : cases + 1], keepdims=True) / norm


def shift_kernel(gram_ref, shift_ref):
    shift_ref[...] = jnp.broadcast_to(rayleigh(gram_ref[...]), shift_ref.shape)


def combine_kernel(first, vector_ref, diagonal_ref, shift_ref, *refs):
    sums, (next_ref, plain_ref, wide_ref) = refs[:-3], refs[-3:]
    vector = vector_ref[...]
    shift = rayleigh(shift_ref[...]) if first else shift_ref[0:1, 0:1]
    following = (diagonal_ref[...] - shift) * vector + off_diagonal(sums)
    next_ref[...] = following
    cross = contract(vector, following, ((1,), (1,)), HIGHEST)
    square = contract(following, following, ((1,), (1,)), HIGHEST)
    put_vector(following, jnp.concatenate([cross, square], axis=1), plain_ref, wide_ref)


def last_gram_kernel(both_ref, *refs):
    messages, total_ref = refs[:-1], refs[-1]
    cases = both_ref.shape[0]
    total = both_ref[...]
    for ref in messages:
        total = total + get_gram(ref, ref.shape[1] - PIECES * cases, cases)
    total_ref[...] = total


def solve(*pairs, panel=8):
    size = pairs[0][0].shape[0]
    works = [jnp.concatenate(pair, axis=1) for pair in pairs]
    shape = works[0].shape
    row = lax.broadcasted_iota(jnp.int32, shape, 0)
    for start in range(0, size, panel):
        pivots = range(start, start + panel)
        spread = [[jnp.broadcast_to(w[:, k : k + 1], shape) for k in pivots] for w in works]
        for k in pivots:
            for n, columns in enumerate(spread):
                pivot = columns[0]
                inverse = 1.0 / pivot[k : k + 1, :]

                def eliminate(matrix):
                    pivot_row = matrix[k : k + 1, :] * inverse
                    return jnp.where(row == k, pivot_row, matrix - pivot * pivot_row)

                works[n] = eliminate(works[n])
                spread[n] = [eliminate(column) for column in columns[1:]]
    return [work[:, size:] for work in works]


def identity(size):
    row = lax.broadcasted_iota(jnp.int32, (size, size), 0)
    column = lax.broadcasted_iota(jnp.int32, (size, size), 1)
    return jnp.where(row == column, 1.0, 0.0)


def first_coefficients_kernel(shift_ref, gram0_ref, gram1_ref, out_ref):
    cases = gram0_ref.shape[0]
    shift = shift_ref[0:1, 0:1]
    bb = gram0_ref[:, :cases]
    bu, uu = gram1_ref[:, :cases], gram1_ref[:, cases:]
    one = identity(cases)
    alpha0, inverse = solve((shift * bb + symmetric(bu), bb), (bb, one))
    r_b = one - shift * alpha0
    r = jnp.concatenate([r_b, -alpha0], axis=0)
    gram = jnp.concatenate(
        [jnp.concatenate([bb, bu], axis=1), jnp.concatenate([bu.T, uu], axis=1)], axis=0
    )
    rr1 = symmetric(mul_t(r, mul(gram, r)))
    d_b = r_b + mul(inverse, rr1)
    out_ref[...] = jnp.concatenate([alpha0, rr1, r_b, d_b], axis=1)


def stack(*parts):
    return jnp.concatenate(parts, axis=0)


def side(*parts):
    return jnp.concatenate(parts, axis=1)


def basis_gram(gram0_ref, gram1_ref, gram2_ref):
    cases = gram0_ref.shape[0]
    bb = gram0_ref[:, :cases]
    bu, uu = gram1_ref[:, :cases], gram1_ref[:, cases:]
    uv, vv = gram2_ref[:, :cases], gram2_ref[:, cases:]
    return stack(side(bb, bu, uu), side(bu.T, uu, uv), side(uu, uv.T, vv))


def directions(shift_ref, first_ref):
    cases = first_ref.shape[0]
    shift = shift_ref[0:1, 0:1]
    alpha0, _, r_b, d_b = [first_ref[:, k * cases : (k + 1) * cases] for k in range(4)]
    zero = jnp.zeros_like(alpha0)
    r1 = stack(r_b, -alpha0, zero)
    d1 = stack(d_b, -alpha0, zero)
    return r1, d1, stack(shift * d_b, d_b - shift * alpha0, -alpha0)


def second_solve_kernel(shift_ref, gram0_ref, gram1_ref, gram2_ref, first_ref, out_ref):
    cases = first_ref.shape[0]
    gram = basis_gram(gram0_ref, gram1_ref, gram2_ref)
    rr1 = first_ref[:, cases : 2 * cases]
    _, d1, s1 = directions(shift_ref, first_ref)
    curvature1 = symmetric(mul_t(d1, mul(gram, s1)))
    out_ref[...] = side(*solve((curvature1, rr1), (rr1, identity(cases))))


def second_coefficients_kernel(
    shift_ref, gram0_ref, gram1_ref, gram2_ref, first_ref, solve_ref, big_ref, small_ref
):
    cases = first_ref.shape[0]
    shift = shift_ref[0:1, 0:1]
    gram = basis_gram(gram0_ref, gram1_ref, gram2_ref)
    r1, d1, s1 = directions(shift_ref, first_ref)
    alpha1, inverse = solve_ref[:, :cases], solve_ref[:, cases:]
    uu = gram1_ref[:, cases:]
    uv, vv = gram2_ref[:, :cases], gram2_ref[:, cases:]
    r2 = r1 - mul(s1, alpha1)
    rr2 = symmetric(mul_t(r2, mul(gram, r2)))
    d2 = r2 + mul(d1, mul(inverse, rr2))
    d2_b, d2_u, d2_v = d2[:cases], d2[cases : 2 * cases], d2[2 * cases :]
    s2 = stack(shift * d2_b, d2_b + shift * d2_u, d2_u)
    with_y = mul_t(d2_b, uv + shift * uu) + mul_t(d2_u, vv + shift * uv)
    curvature2 = mul_t(d2, mul(gram, s2)) + mul(with_y, d2_v)
    zero = jnp.zeros_like(uu)
    x2 = stack(first_ref[:, :cases], zero, zero) + mul(d1, alpha1)
    small_ref[...] = side(curvature2, rr2, d2_v, zero)
    big_ref[...] = side(d2, r2, s2, x2)


def vectors_kernel(big_ref, b_ref, u_ref, v_ref, vectors_ref):
    basis = jnp.concatenate([b_ref[...], u_ref[...], v_ref[...]], axis=0)
    vectors_ref[...] = mul_t(big_ref[...], basis)


def finish_kernel(vectors_ref, small_ref, both_ref, other_ref, v_ref, diagonal_ref, *refs):
    sums, (solution_ref, residual_ref) = refs[:-2], refs[-2:]
    cases = v_ref.shape[0]
    d2, r2, s2, x2 = [vectors_ref[k * cases : (k + 1) * cases, :] for k in range(4)]
    curvature2, rr2, d2_v = [small_ref[:, k * cases : (k + 1) * cases] for k in range(3)]
    both = symmetric(both_ref[...] + other_ref[...])
    curvature2 = symmetric(curvature2 + mul_t(d2_v, mul(both, d2_v)))
    (alpha2,) = solve((curvature2, rr2), panel=16)
    y = diagonal_ref[...] * v_ref[...] + off_diagonal(sums)
    s2 = s2 + mul_t(d2_v, y)
    solution_ref[...] = x2 + mul_t(alpha2, d2)
    residual_ref[...] = r2 - mul_t(alpha2, s2)


def call(kernel, name, outs, *args, scratch=(), scalars=(), far=(), cost=0, room=VMEM_BYTES):
    spaces = {**dict.fromkeys(scalars, smem), **dict.fromkeys(far, hbm)}
    return pl.pallas_call(
        kernel,
        out_shape=outs,
        in_specs=[spaces.get(k, vmem) for k in range(len(args))],
        out_specs=jax.tree.map(lambda _: vmem, outs),
        scratch_shapes=list(scratch),
        compiler_params=pltpu.CompilerParams(vmem_limit_bytes=room),
        cost_estimate=pl.CostEstimate(flops=int(cost * 1e9), bytes_accessed=0, transcendentals=0),
        name=name,
    )(*args)


def local(
    right_side,
    self_term,
    near_tiles,
    near_rows,
    near_cols,
    near_count,
    far_left,
    far_right,
    far_rows,
    far_cols,
    far_rank,
):
    cases, width = right_side.shape
    leaf = near_tiles.shape[-1]
    per = width // leaf
    rows, cols = lax.axis_size("row"), lax.axis_size("col")
    chips = cols // 2
    slots = near_tiles.shape[2] + far_left.shape[2]
    long = width + PIECES * GRAM
    table = jnp.concatenate(
        [
            jnp.stack([lax.axis_index("row"), lax.axis_index("col")]).astype(jnp.int32),
            near_rows[0, 0],
            far_rows[0, 0],
            near_cols[0, 0],
            far_cols[0, 0],
            far_rank[0, 0],
            near_count[0],
        ]
    )
    diagonal = self_term[None, :]
    tiles, turned = call(
        dense_kernel,
        "dense_tiles",
        [bf16(slots, leaf, leaf)] * 2,
        table,
        near_tiles[0, 0],
        far_left[0, 0],
        far_right[0, 0],
        scalars=(0,),
        far=(1, 2, 3),
        room=DENSE_BYTES,
        scratch=[
            pltpu.VMEM(far_left.shape[2:], jnp.bfloat16),
            pltpu.VMEM(far_right.shape[2:], jnp.bfloat16),
            pltpu.SemaphoreType.DMA((3,)),
        ],
    )

    def apply(plain, wide, last=(), beside=()):
        over_row = [partner_permute(wide, "row", k) for k in range(1, rows)]
        over_chip, flip = [], 1
        while flip < chips:
            over_chip += [partner_permute(m, "col", 2 * flip) for m in [plain, *over_chip]]
            flip *= 2
        send, keep, gram = call(
            rows_kernel,
            "rows_half",
            [bf16(chips + 1, cases, width), f32(chips, cases, width), f32(cases, GRAM)],
            table,
            turned,
            wide,
            *over_row,
            scalars=(0,),
            scratch=[
                pltpu.VMEM((rows * per, cases, leaf), jnp.bfloat16),
                pltpu.VMEM((cols * per, cases, leaf), jnp.float32),
            ],
        )
        over_chip, beside, send, keep = lax.optimization_barrier((over_chip, beside, send, keep))
        got = partner_permute(send, "col", 1)
        own_chip, gram, *row_messages = call(
            pair_kernel,
            "pair_sums",
            [f32(cases, width), f32(cases, GRAM)] + [bf16(cases, long)] * (chips - 1),
            table,
            keep,
            gram,
            got,
            scalars=(0,),
        )
        from_chips = [partner_permute(m, "col", 2 * k) for k, m in enumerate(row_messages, 1)]
        other_core = [partner_permute(v, "col", 1) for v in [plain] + over_chip]
        own_row, gram = call(
            chip_sums_kernel,
            "chip_sums",
            [f32(cases, width), f32(cases, GRAM)],
            own_chip,
            gram,
            *from_chips,
            cost=1,
        )
        row_group = [None] * cols
        for k, (a, b) in enumerate(zip([plain] + over_chip, other_core)):
            row_group[2 * k], row_group[2 * k + 1] = a, b
        behind = PIECES * cases if last else 0
        own_col, *outs = call(
            functools.partial(cols_kernel, rows, cols),
            "cols_half",
            [f32(cases, width)]
            + [bf16(cases, width + behind)] * (rows - 1)
            + [f32(cases, cases)] * bool(last),
            table,
            tiles,
            *row_group,
            *([wide, *over_row, *last] if last else []),
            scalars=(0,),
            scratch=[
                pltpu.VMEM((cols * per, cases, leaf), jnp.bfloat16),
                pltpu.VMEM((rows * per, cases, leaf), jnp.float32),
            ],
        )
        from_rows = [partner_permute(m, "row", k) for k, m in enumerate(outs[: rows - 1], 1)]
        if not last:
            return [own_row, own_col, *from_rows], gram
        solved = call(
            second_solve_kernel, "solve", f32(cases, 2 * cases), shift, gram0, gram1, gram, beside
        )
        from_rows, solved = lax.optimization_barrier((from_rows, solved))
        both = call(last_gram_kernel, "last_gram", f32(cases, cases), outs[-1], *from_rows)
        return [own_row, own_col, *from_rows], gram, both, beside, solved

    def advance(first, vector, shift, sums):
        return call(
            functools.partial(combine_kernel, first),
            "combine",
            [f32(cases, width), bf16(cases, width), bf16(cases, long)],
            vector,
            diagonal,
            shift,
            *sums,
        )

    b = right_side
    plain, wide = call(
        first_kernel, "first_message", [bf16(cases, width), bf16(cases, long)], b, diagonal, cost=10
    )
    sums, gram0 = apply(plain, wide)
    u, plain, wide = advance(True, b, gram0, sums)
    shift = call(shift_kernel, "shift", f32(8, 128), gram0)
    sums, gram1 = apply(plain, wide)
    v, plain, wide = advance(False, u, shift, sums)
    first = call(
        first_coefficients_kernel, "coefficients", f32(cases, 4 * cases), shift, gram0, gram1
    )
    sums, gram2, both, first, solved = apply(plain, wide, last=(v, diagonal), beside=first)
    over_chip = [partner_permute(both, "col", 2 * k) for k in range(1, chips)]
    big, small = call(
        second_coefficients_kernel,
        "coefficients",
        [f32(3 * cases, 4 * cases), f32(cases, 4 * cases)],
        shift,
        gram0,
        gram1,
        gram2,
        first,
        solved,
    )
    over_chip, big = lax.optimization_barrier((over_chip, big))
    both = functools.reduce(jnp.add, over_chip, both)
    other = partner_permute(both, "col", 1)
    big, _ = lax.optimization_barrier((big, both))
    vectors = call(vectors_kernel, "vectors", f32(4 * cases, width), big, b, u, v)
    other, vectors = lax.optimization_barrier((other, vectors))
    return call(
        finish_kernel,
        "finish",
        [f32(cases, width), f32(cases, width)],
        vectors,
        small,
        both,
        other,
        v,
        diagonal,
        *sums,
    )


def solution(mesh):
    in_specs = (
        P(None, ("row", "col")),
        P(("row", "col")),
        P("row", "col", None, None, None),
        P("row", "col", None),
        P("row", "col", None),
        P("row", "col"),
        P("row", "col", None, None, None),
        P("row", "col", None, None, None),
        P("row", "col", None),
        P("row", "col", None),
        P("row", "col", None),
    )
    out_specs = (P(None, ("row", "col")), P(None, ("row", "col")))
    return jax.shard_map(local, mesh=mesh, in_specs=in_specs, out_specs=out_specs, check_vma=False)
```

```python
import functools

import jax
import jax.numpy as jnp
from jax import lax
from jax.experimental import pallas as pl
from jax.experimental.pallas import tpu as pltpu
from jax.sharding import PartitionSpec as P

VMEM_BYTES = 24 * 1024 * 1024
DENSE_BYTES = 24 * 1024 * 1024
HIGHEST = lax.Precision.HIGHEST
GRAM = 128
PIECES = 2
UNROLL = 32

vmem = pl.BlockSpec(memory_space=pltpu.VMEM)
smem = pl.BlockSpec(memory_space=pltpu.SMEM)
hbm = pl.BlockSpec(memory_space=pltpu.HBM)


def f32(*shape):
    return jax.ShapeDtypeStruct(shape, jnp.float32)


def bf16(*shape):
    return jax.ShapeDtypeStruct(shape, jnp.bfloat16)


def contract(left, right, dims, precision=None):
    return lax.dot_general(
        left, right, (dims, ((), ())), precision=precision, preferred_element_type=jnp.float32
    )


def mul(left, right):
    return contract(left, right, ((1,), (0,)), HIGHEST)


def mul_t(left, right):
    return contract(left, right, ((0,), (0,)), HIGHEST)


def symmetric(matrix):
    return 0.5 * (matrix + matrix.T)


def partner_permute(value, axis, flip):
    size = lax.axis_size(axis)
    return lax.ppermute(value, axis, [(i, i ^ flip) for i in range(size)])


def put_gram(ref, first, gram):
    columns = gram.shape[1]
    for k in range(PIECES):
        piece = gram.astype(jnp.bfloat16)
        ref[:, first + k * columns : first + (k + 1) * columns] = piece
        gram = gram - piece.astype(jnp.float32)


def get_gram(ref, first, columns):
    parts = [
        ref[:, first + k * columns : first + (k + 1) * columns].astype(jnp.float32)
        for k in range(PIECES)
    ]
    return functools.reduce(jnp.add, reversed(parts))


def dense_kernel(
    table, near_ref, left_ref, right_ref, tile_ref, turned_ref, lefts, rights, sems
):
    near_slots, far_slots = near_ref.shape[0], left_ref.shape[0]
    ranks = 2 + 2 * (near_slots + far_slots)
    count = table[ranks + far_slots]
    copies = [
        pltpu.make_async_copy(source, target, sems.at[k])
        for k, (source, target) in enumerate(
            [
                (left_ref, lefts),
                (right_ref, rights),
                (near_ref, tile_ref.at[pl.ds(0, near_slots)]),
            ]
        )
    ]
    for copy in copies:
        copy.start()
    copies[0].wait()
    copies[1].wait()

    def far(s, _):
        row = lax.broadcasted_iota(jnp.int32, lefts.shape[1:], 0)
        left = jnp.where(row < table[ranks + s], lefts[s].astype(jnp.float32), 0.0)
        left, right = left.astype(jnp.bfloat16), rights[s]
        tile_ref[near_slots + s] = contract(left, right, ((0,), (0,))).astype(jnp.bfloat16)
        turned_ref[near_slots + s] = contract(right, left, ((0,), (0,))).astype(jnp.bfloat16)
        return 0

    def near(s, _):
        tile = tile_ref[s]
        tile = jnp.where(s < count, tile, jnp.zeros_like(tile))
        tile_ref[s] = tile
        turned_ref[s] = tile.T
        return 0

    lax.fori_loop(0, far_slots, far, 0, unroll=16)
    copies[2].wait()
    lax.fori_loop(0, near_slots, near, 0, unroll=8)


def tile_sums(table, inputs, outputs, tile_ref, cells, total):
    total[...] = jnp.zeros_like(total)

    def step(s, _):
        product = contract(cells[table[inputs + s]], tile_ref[s], ((1,), (0,)))
        to = table[outputs + s]
        total[to] = total[to] + product
        return 0

    lax.fori_loop(0, tile_ref.shape[0], step, 0, unroll=UNROLL)


def place(block, ref, cells, per):
    leaf = cells.shape[-1]
    for j in range(per):
        cells[block * per + j] = ref[:, j * leaf : (j + 1) * leaf]


def rows_kernel(table, tile_ref, *refs):
    blocks, (send_ref, keep_ref, gram_ref, cells, total) = refs[:-5], refs[-5:]
    chips, _, width = keep_ref.shape
    leaf = cells.shape[-1]
    per = width // leaf
    me, core = table[0], table[1] % 2
    for flip, ref in enumerate(blocks):
        place(me ^ flip, ref, cells, per)
    slots = tile_ref.shape[0]
    tile_sums(table, 2 + slots, 2, tile_ref, cells, total)
    for z in range(chips):
        for j in range(per):
            part = slice(j * leaf, (j + 1) * leaf)
            send_ref[z, :, part] = total[(2 * z + 1 - core) * per + j].astype(jnp.bfloat16)
            keep_ref[z, :, part] = total[(2 * z + core) * per + j]
    gram = functools.reduce(jnp.add, [get_gram(ref, width, GRAM) for ref in blocks])
    gram_ref[...] = gram
    send_ref[chips] = jnp.zeros(send_ref.shape[1:], send_ref.dtype)
    put_gram(send_ref.at[chips], 0, gram)


def cols_kernel(rows, cols, table, tile_ref, *refs):
    blocks, refs, (cells, total) = refs[:cols], refs[cols:-2], refs[-2:]
    last = refs[: rows + 2] if len(refs) > rows else ()
    outs = refs[len(last) : len(last) + rows]
    width = outs[0].shape[1]
    leaf = cells.shape[-1]
    per = width // leaf
    me = table[0]
    for flip, ref in enumerate(blocks):
        place(table[1] ^ flip, ref, cells, per)
    slots = tile_ref.shape[0]
    tile_sums(table, 2, 2 + slots, tile_ref, cells, total)
    for flip, out in enumerate(outs):
        for j in range(per):
            part = total[(me ^ flip) * per + j]
            out[:, j * leaf : (j + 1) * leaf] = part.astype(out.dtype)
    if last:
        vector_ref, diagonal_ref = last[rows:]
        vector = vector_ref[...]
        both = contract(vector, vector * diagonal_ref[...], ((1,), (1,)), HIGHEST)
        half = jnp.zeros_like(both)
        for flip, ref in enumerate(last[:rows]):
            for j in range(per):
                cluster = ref[:, j * leaf : (j + 1) * leaf]
                image = total[(me ^ flip) * per + j].astype(jnp.bfloat16)
                half = half + contract(cluster, image, ((1,), (1,)))
        both = both + 2.0 * half
        refs[-1][...] = both
        for out in outs[1:]:
            put_gram(out, width, both)


def pair_kernel(table, keep_ref, gram_ref, got_ref, own_ref, own_gram_ref, *messages):
    chips, _, width = keep_ref.shape
    chip = table[1] // 2
    gram = gram_ref[...] + get_gram(got_ref.at[chips], 0, GRAM)
    own_gram_ref[...] = gram
    for flip, out in enumerate((own_ref, *messages)):
        z = chip ^ flip
        out[:, :width] = (keep_ref[z] + got_ref[z].astype(jnp.float32)).astype(out.dtype)
    for out in messages:
        put_gram(out, width, gram)


def chip_sums_kernel(own_ref, gram_ref, *refs):
    messages, (out_ref, total_ref) = refs[:-2], refs[-2:]
    width = own_ref.shape[1]
    total, gram = own_ref[...], gram_ref[...]
    for ref in messages:
        total = total + ref[:, :width].astype(jnp.float32)
        gram = gram + get_gram(ref, width, GRAM)
    out_ref[...] = total
    total_ref[...] = gram


def put_vector(vector, gram, plain_ref, wide_ref):
    rounded = vector.astype(jnp.bfloat16)
    width = vector.shape[1]
    plain_ref[...] = rounded
    wide_ref[:, :width] = rounded
    put_gram(wide_ref, width, gram)


def first_kernel(vector_ref, diagonal_ref, plain_ref, wide_ref):
    vector = vector_ref[...]
    gram = contract(vector, vector, ((1,), (1,)), HIGHEST)
    weighted = jnp.sum(vector * vector * diagonal_ref[...], axis=1, keepdims=True)
    gram = jnp.concatenate([gram, jnp.broadcast_to(weighted, gram.shape)], axis=1)
    put_vector(vector, gram, plain_ref, wide_ref)


def off_diagonal(refs):
    width = refs[0].shape[1]
    total = refs[0][...] + refs[1][...]
    for ref in refs[2:]:
        total = total + ref[:, :width].astype(jnp.float32)
    return total


def shift_kernel(gram_ref, shift_ref):
    gram = gram_ref[...]
    cases = gram.shape[0]
    norm = jnp.sum(identity(cases) * gram[:, :cases], keepdims=True)
    quotient = jnp.sum(gram[:, cases : cases + 1], keepdims=True) / norm
    shift_ref[...] = jnp.broadcast_to(quotient, shift_ref.shape)


def combine_kernel(vector_ref, diagonal_ref, shift_ref, *refs):
    sums, (next_ref, plain_ref, wide_ref) = refs[:-3], refs[-3:]
    vector = vector_ref[...]
    shift = shift_ref[0:1, 0:1]
    following = (diagonal_ref[...] - shift) * vector + off_diagonal(sums)
    next_ref[...] = following
    cross = contract(vector, following, ((1,), (1,)), HIGHEST)
    square = contract(following, following, ((1,), (1,)), HIGHEST)
    put_vector(following, jnp.concatenate([cross, square], axis=1), plain_ref, wide_ref)


def last_gram_kernel(both_ref, *refs):
    messages, total_ref = refs[:-1], refs[-1]
    cases = both_ref.shape[0]
    total = both_ref[...]
    for ref in messages:
        total = total + get_gram(ref, ref.shape[1] - PIECES * cases, cases)
    total_ref[...] = total


def solve(*pairs, panel=8):
    size = pairs[0][0].shape[0]
    works = [jnp.concatenate(pair, axis=1) for pair in pairs]
    shape = works[0].shape
    row = lax.broadcasted_iota(jnp.int32, shape, 0)
    for start in range(0, size, panel):
        pivots = range(start, start + panel)
        spread = [[jnp.broadcast_to(w[:, k : k + 1], shape) for k in pivots] for w in works]
        for k in pivots:
            for n, columns in enumerate(spread):
                pivot = columns[0]
                inverse = 1.0 / pivot[k : k + 1, :]

                def eliminate(matrix):
                    pivot_row = matrix[k : k + 1, :] * inverse
                    return jnp.where(row == k, pivot_row, matrix - pivot * pivot_row)

                works[n] = eliminate(works[n])
                spread[n] = [eliminate(column) for column in columns[1:]]
    return [work[:, size:] for work in works]


def identity(size):
    row = lax.broadcasted_iota(jnp.int32, (size, size), 0)
    column = lax.broadcasted_iota(jnp.int32, (size, size), 1)
    return jnp.where(row == column, 1.0, 0.0)


def first_coefficients_kernel(shift_ref, gram0_ref, gram1_ref, out_ref):
    cases = gram0_ref.shape[0]
    shift = shift_ref[0:1, 0:1]
    bb = gram0_ref[:, :cases]
    bu, uu = gram1_ref[:, :cases], gram1_ref[:, cases:]
    one = identity(cases)
    alpha0, inverse = solve((shift * bb + symmetric(bu), bb), (bb, one))
    r_b = one - shift * alpha0
    r = jnp.concatenate([r_b, -alpha0], axis=0)
    gram = jnp.concatenate(
        [jnp.concatenate([bb, bu], axis=1), jnp.concatenate([bu.T, uu], axis=1)], axis=0
    )
    rr1 = symmetric(mul_t(r, mul(gram, r)))
    d_b = r_b + mul(inverse, rr1)
    out_ref[...] = jnp.concatenate([alpha0, rr1, r_b, d_b], axis=1)


def stack(*parts):
    return jnp.concatenate(parts, axis=0)


def side(*parts):
    return jnp.concatenate(parts, axis=1)


def basis_gram(gram0_ref, gram1_ref, gram2_ref):
    cases = gram0_ref.shape[0]
    bb = gram0_ref[:, :cases]
    bu, uu = gram1_ref[:, :cases], gram1_ref[:, cases:]
    uv, vv = gram2_ref[:, :cases], gram2_ref[:, cases:]
    return stack(side(bb, bu, uu), side(bu.T, uu, uv), side(uu, uv.T, vv))


def directions(shift_ref, first_ref):
    cases = first_ref.shape[0]
    shift = shift_ref[0:1, 0:1]
    alpha0, _, r_b, d_b = [first_ref[:, k * cases : (k + 1) * cases] for k in range(4)]
    zero = jnp.zeros_like(alpha0)
    r1 = stack(r_b, -alpha0, zero)
    d1 = stack(d_b, -alpha0, zero)
    return r1, d1, stack(shift * d_b, d_b - shift * alpha0, -alpha0)


def second_solve_kernel(shift_ref, gram0_ref, gram1_ref, gram2_ref, first_ref, out_ref):
    cases = first_ref.shape[0]
    gram = basis_gram(gram0_ref, gram1_ref, gram2_ref)
    rr1 = first_ref[:, cases : 2 * cases]
    _, d1, s1 = directions(shift_ref, first_ref)
    curvature1 = symmetric(mul_t(d1, mul(gram, s1)))
    out_ref[...] = side(*solve((curvature1, rr1), (rr1, identity(cases))))


def second_coefficients_kernel(
    shift_ref, gram0_ref, gram1_ref, gram2_ref, first_ref, solve_ref, big_ref, small_ref
):
    cases = first_ref.shape[0]
    shift = shift_ref[0:1, 0:1]
    gram = basis_gram(gram0_ref, gram1_ref, gram2_ref)
    r1, d1, s1 = directions(shift_ref, first_ref)
    alpha1, inverse = solve_ref[:, :cases], solve_ref[:, cases:]
    uu = gram1_ref[:, cases:]
    uv, vv = gram2_ref[:, :cases], gram2_ref[:, cases:]
    r2 = r1 - mul(s1, alpha1)
    rr2 = symmetric(mul_t(r2, mul(gram, r2)))
    d2 = r2 + mul(d1, mul(inverse, rr2))
    d2_b, d2_u, d2_v = d2[:cases], d2[cases : 2 * cases], d2[2 * cases :]
    s2 = stack(shift * d2_b, d2_b + shift * d2_u, d2_u)
    with_y = mul_t(d2_b, uv + shift * uu) + mul_t(d2_u, vv + shift * uv)
    curvature2 = mul_t(d2, mul(gram, s2)) + mul(with_y, d2_v)
    zero = jnp.zeros_like(uu)
    x2 = stack(first_ref[:, :cases], zero, zero) + mul(d1, alpha1)
    small_ref[...] = side(curvature2, rr2, d2_v, zero)
    big_ref[...] = side(d2, r2, s2, x2)


def vectors_kernel(big_ref, b_ref, u_ref, v_ref, vectors_ref):
    basis = jnp.concatenate([b_ref[...], u_ref[...], v_ref[...]], axis=0)
    vectors_ref[...] = mul_t(big_ref[...], basis)


def finish_kernel(vectors_ref, small_ref, both_ref, other_ref, v_ref, diagonal_ref, *refs):
    sums, (solution_ref, residual_ref) = refs[:-2], refs[-2:]
    cases = v_ref.shape[0]
    d2, r2, s2, x2 = [vectors_ref[k * cases : (k + 1) * cases, :] for k in range(4)]
    curvature2, rr2, d2_v = [small_ref[:, k * cases : (k + 1) * cases] for k in range(3)]
    both = symmetric(both_ref[...] + other_ref[...])
    curvature2 = symmetric(curvature2 + mul_t(d2_v, mul(both, d2_v)))
    (alpha2,) = solve((curvature2, rr2), panel=16)
    y = diagonal_ref[...] * v_ref[...] + off_diagonal(sums)
    s2 = s2 + mul_t(d2_v, y)
    solution_ref[...] = x2 + mul_t(alpha2, d2)
    residual_ref[...] = r2 - mul_t(alpha2, s2)


def call(kernel, name, outs, *args, scratch=(), scalars=(), far=(), cost=0, room=VMEM_BYTES):
    spaces = {**dict.fromkeys(scalars, smem), **dict.fromkeys(far, hbm)}
    return pl.pallas_call(
        kernel,
        out_shape=outs,
        in_specs=[spaces.get(k, vmem) for k in range(len(args))],
        out_specs=jax.tree.map(lambda _: vmem, outs),
        scratch_shapes=list(scratch),
        compiler_params=pltpu.CompilerParams(vmem_limit_bytes=room),
        cost_estimate=pl.CostEstimate(flops=int(cost * 1e9), bytes_accessed=0, transcendentals=0),
        name=name,
    )(*args)


def local(
    right_side,
    self_term,
    near_tiles,
    near_rows,
    near_cols,
    near_count,
    far_left,
    far_right,
    far_rows,
    far_cols,
    far_rank,
):
    cases, width = right_side.shape
    leaf = near_tiles.shape[-1]
    per = width // leaf
    rows, cols = lax.axis_size("row"), lax.axis_size("col")
    chips = cols // 2
    slots = near_tiles.shape[2] + far_left.shape[2]
    long = width + PIECES * GRAM
    table = jnp.concatenate(
        [
            jnp.stack([lax.axis_index("row"), lax.axis_index("col")]).astype(jnp.int32),
            near_rows[0, 0],
            far_rows[0, 0],
            near_cols[0, 0],
            far_cols[0, 0],
            far_rank[0, 0],
            near_count[0],
        ]
    )
    diagonal = self_term[None, :]
    tiles, turned = call(
        dense_kernel,
        "dense_tiles",
        [bf16(slots, leaf, leaf)] * 2,
        table,
        near_tiles[0, 0],
        far_left[0, 0],
        far_right[0, 0],
        scalars=(0,),
        far=(1, 2, 3),
        room=DENSE_BYTES,
        scratch=[
            pltpu.VMEM(far_left.shape[2:], jnp.bfloat16),
            pltpu.VMEM(far_right.shape[2:], jnp.bfloat16),
            pltpu.SemaphoreType.DMA((3,)),
        ],
    )

    def apply(plain, wide, during, last=()):
        over_row = [partner_permute(wide, "row", k) for k in range(1, rows)]
        held, flip = {0: plain}, chips // 2
        while flip:
            held |= {k ^ flip: partner_permute(m, "col", 2 * flip) for k, m in held.items()}
            flip //= 2
        over_chip = [held[k] for k in range(1, chips)]
        send, keep, gram = call(
            rows_kernel,
            "rows_half",
            [bf16(chips + 1, cases, width), f32(chips, cases, width), f32(cases, GRAM)],
            table,
            turned,
            wide,
            *over_row,
            scalars=(0,),
            scratch=[
                pltpu.VMEM((rows * per, cases, leaf), jnp.bfloat16),
                pltpu.VMEM((cols * per, cases, leaf), jnp.float32),
            ],
        )
        over_chip, send, keep = lax.optimization_barrier((over_chip, send, keep))
        got = partner_permute(send, "col", 1)
        other_core = [partner_permute(v, "col", 1) for v in [plain] + over_chip]
        got, other_core = lax.optimization_barrier((got, other_core))
        own_chip, gram, *row_messages = call(
            pair_kernel,
            "pair_sums",
            [f32(cases, width), f32(cases, GRAM)] + [bf16(cases, long)] * (chips - 1),
            table,
            keep,
            gram,
            got,
            scalars=(0,),
        )
        from_chips = [partner_permute(m, "col", 2 * k) for k, m in enumerate(row_messages, 1)]
        own_row, gram = call(
            chip_sums_kernel,
            "chip_sums",
            [f32(cases, width), f32(cases, GRAM)],
            own_chip,
            gram,
            *from_chips,
            cost=1,
        )
        row_group = [None] * cols
        for k, (a, b) in enumerate(zip([plain] + over_chip, other_core)):
            row_group[2 * k], row_group[2 * k + 1] = a, b
        behind = PIECES * cases if last else 0
        own_col, *outs = call(
            functools.partial(cols_kernel, rows, cols),
            "cols_half",
            [f32(cases, width)]
            + [bf16(cases, width + behind)] * (rows - 1)
            + [f32(cases, cases)] * bool(last),
            table,
            tiles,
            *row_group,
            *([wide, *over_row, *last] if last else []),
            scalars=(0,),
            scratch=[
                pltpu.VMEM((cols * per, cases, leaf), jnp.bfloat16),
                pltpu.VMEM((rows * per, cases, leaf), jnp.float32),
            ],
        )
        from_rows = [partner_permute(m, "row", k) for k, m in enumerate(outs[: rows - 1], 1)]
        made = during(gram)
        from_rows, made = lax.optimization_barrier((from_rows, made))
        sums = [own_row, own_col, *from_rows]
        if not last:
            return sums, gram, made
        both = call(last_gram_kernel, "last_gram", f32(cases, cases), outs[-1], *from_rows)
        return sums, gram, made, both

    def advance(vector, shift, sums):
        return call(
            combine_kernel,
            "combine",
            [f32(cases, width), bf16(cases, width), bf16(cases, long)],
            vector,
            diagonal,
            shift,
            *sums,
        )

    b = right_side
    plain, wide = call(
        first_kernel, "first_message", [bf16(cases, width), bf16(cases, long)], b, diagonal, cost=10
    )
    sums, gram0, shift = apply(
        plain, wide, lambda gram: call(shift_kernel, "shift", f32(8, 128), gram)
    )
    u, plain, wide = advance(b, shift, sums)
    sums, gram1, first = apply(
        plain,
        wide,
        lambda gram: call(
            first_coefficients_kernel, "coefficients", f32(cases, 4 * cases), shift, gram0, gram
        ),
    )
    v, plain, wide = advance(u, shift, sums)
    sums, gram2, solved, both = apply(
        plain,
        wide,
        lambda gram: call(
            second_solve_kernel, "solve", f32(cases, 2 * cases), shift, gram0, gram1, gram, first
        ),
        last=(v, diagonal),
    )
    over_chip = [partner_permute(both, "col", 2 * k) for k in range(1, chips)]
    big, small = call(
        second_coefficients_kernel,
        "coefficients",
        [f32(3 * cases, 4 * cases), f32(cases, 4 * cases)],
        shift,
        gram0,
        gram1,
        gram2,
        first,
        solved,
    )
    over_chip, big = lax.optimization_barrier((over_chip, big))
    both = functools.reduce(jnp.add, over_chip, both)
    other = partner_permute(both, "col", 1)
    big, _ = lax.optimization_barrier((big, both))
    vectors = call(vectors_kernel, "vectors", f32(4 * cases, width), big, b, u, v)
    other, vectors = lax.optimization_barrier((other, vectors))
    return call(
        finish_kernel,
        "finish",
        [f32(cases, width), f32(cases, width)],
        vectors,
        small,
        both,
        other,
        v,
        diagonal,
        *sums,
    )


def solution(mesh):
    in_specs = (
        P(None, ("row", "col")),
        P(("row", "col")),
        P("row", "col", None, None, None),
        P("row", "col", None),
        P("row", "col", None),
        P("row", "col"),
        P("row", "col", None, None, None),
        P("row", "col", None, None, None),
        P("row", "col", None),
        P("row", "col", None),
        P("row", "col", None),
    )
    out_specs = (P(None, ("row", "col")), P(None, ("row", "col")))
    return jax.shard_map(local, mesh=mesh, in_specs=in_specs, out_specs=out_specs, check_vma=False)
```

```python
import functools

import jax
import jax.numpy as jnp
from jax import lax
from jax.experimental import pallas as pl
from jax.experimental.pallas import tpu as pltpu
from jax.sharding import PartitionSpec as P

VMEM_BYTES = 24 * 1024 * 1024
HIGHEST = lax.Precision.HIGHEST
GRAM = 128
PIECES = 2
UNROLL = 96

vmem = pl.BlockSpec(memory_space=pltpu.VMEM)
smem = pl.BlockSpec(memory_space=pltpu.SMEM)


def f32(*shape):
    return jax.ShapeDtypeStruct(shape, jnp.float32)


def bf16(*shape):
    return jax.ShapeDtypeStruct(shape, jnp.bfloat16)


def contract(left, right, dims, precision=None):
    return lax.dot_general(
        left, right, (dims, ((), ())), precision=precision, preferred_element_type=jnp.float32
    )


def mul(left, right):
    return contract(left, right, ((1,), (0,)), HIGHEST)


def mul_t(left, right):
    return contract(left, right, ((0,), (0,)), HIGHEST)


def symmetric(matrix):
    return 0.5 * (matrix + matrix.T)


def partner_permute(value, axis, flip):
    size = lax.axis_size(axis)
    return lax.ppermute(value, axis, [(i, i ^ flip) for i in range(size)])


def put_gram(ref, first, gram):
    columns = gram.shape[1]
    for k in range(PIECES):
        piece = gram.astype(jnp.bfloat16)
        ref[:, first + k * columns : first + (k + 1) * columns] = piece
        gram = gram - piece.astype(jnp.float32)


def get_gram(ref, first, columns):
    parts = [
        ref[:, first + k * columns : first + (k + 1) * columns].astype(jnp.float32)
        for k in range(PIECES)
    ]
    return functools.reduce(jnp.add, reversed(parts))


def dense_kernel(table, near_ref, left_ref, right_ref, tile_ref, turned_ref):
    near_slots, far_slots = near_ref.shape[0], left_ref.shape[0]
    ranks = 2 + 2 * (near_slots + far_slots)
    count = table[ranks + far_slots]

    def far(s, _):
        row = lax.broadcasted_iota(jnp.int32, left_ref.shape[1:], 0)
        left = jnp.where(row < table[ranks + s], left_ref[s].astype(jnp.float32), 0.0)
        left, right = left.astype(jnp.bfloat16), right_ref[s]
        tile_ref[near_slots + s] = contract(left, right, ((0,), (0,))).astype(jnp.bfloat16)
        turned_ref[near_slots + s] = contract(right, left, ((0,), (0,))).astype(jnp.bfloat16)
        return 0

    def near(s, _):
        tile = near_ref[s]
        tile = jnp.where(s < count, tile, jnp.zeros_like(tile))
        tile_ref[s] = tile
        turned_ref[s] = tile.T
        return 0

    lax.fori_loop(0, far_slots, far, 0, unroll=16)
    lax.fori_loop(0, near_slots, near, 0, unroll=8)


def tile_sums(table, inputs, outputs, tile_ref, cells, total):
    total[...] = jnp.zeros_like(total)

    def step(s, _):
        product = contract(cells[table[inputs + s]], tile_ref[s], ((1,), (0,)))
        to = table[outputs + s]
        total[to] = total[to] + product
        return 0

    lax.fori_loop(0, tile_ref.shape[0], step, 0, unroll=UNROLL)


def place(block, ref, cells, per):
    leaf = cells.shape[-1]
    for j in range(per):
        cells[block * per + j] = ref[:, j * leaf : (j + 1) * leaf]


def rows_kernel(table, tile_ref, *refs):
    blocks, (send_ref, keep_ref, gram_ref, cells, total) = refs[:-5], refs[-5:]
    chips, _, width = keep_ref.shape
    leaf = cells.shape[-1]
    per = width // leaf
    me, core = table[0], table[1] % 2
    for flip, ref in enumerate(blocks):
        place(me ^ flip, ref, cells, per)
    slots = tile_ref.shape[0]
    tile_sums(table, 2 + slots, 2, tile_ref, cells, total)
    for z in range(chips):
        for j in range(per):
            part = slice(j * leaf, (j + 1) * leaf)
            send_ref[z, :, part] = total[(2 * z + 1 - core) * per + j].astype(jnp.bfloat16)
            keep_ref[z, :, part] = total[(2 * z + core) * per + j]
    gram = functools.reduce(jnp.add, [get_gram(ref, width, GRAM) for ref in blocks])
    gram_ref[...] = gram
    send_ref[chips] = jnp.zeros(send_ref.shape[1:], send_ref.dtype)
    put_gram(send_ref.at[chips], 0, gram)


def cols_kernel(rows, cols, table, tile_ref, *refs):
    blocks, refs, (cells, total) = refs[:cols], refs[cols:-2], refs[-2:]
    last = refs[: rows + 2] if len(refs) > rows else ()
    outs = refs[len(last) : len(last) + rows]
    width = outs[0].shape[1]
    leaf = cells.shape[-1]
    per = width // leaf
    me = table[0]
    for flip, ref in enumerate(blocks):
        place(table[1] ^ flip, ref, cells, per)
    slots = tile_ref.shape[0]
    tile_sums(table, 2, 2 + slots, tile_ref, cells, total)
    for flip, out in enumerate(outs):
        for j in range(per):
            part = total[(me ^ flip) * per + j]
            out[:, j * leaf : (j + 1) * leaf] = part.astype(out.dtype)
    if last:
        vector_ref, diagonal_ref = last[rows:]
        vector = vector_ref[...]
        both = contract(vector, vector * diagonal_ref[...], ((1,), (1,)), HIGHEST)
        half = jnp.zeros_like(both)
        for flip, ref in enumerate(last[:rows]):
            for j in range(per):
                cluster = ref[:, j * leaf : (j + 1) * leaf]
                image = total[(me ^ flip) * per + j].astype(jnp.bfloat16)
                half = half + contract(cluster, image, ((1,), (1,)))
        both = both + 2.0 * half
        refs[-1][...] = both
        for out in outs[1:]:
            put_gram(out, width, both)


def pair_kernel(table, keep_ref, gram_ref, got_ref, own_ref, own_gram_ref, *messages):
    chips, _, width = keep_ref.shape
    chip = table[1] // 2
    gram = gram_ref[...] + get_gram(got_ref.at[chips], 0, GRAM)
    own_gram_ref[...] = gram
    for flip, out in enumerate((own_ref, *messages)):
        z = chip ^ flip
        out[:, :width] = (keep_ref[z] + got_ref[z].astype(jnp.float32)).astype(out.dtype)
    for out in messages:
        put_gram(out, width, gram)


def chip_sums_kernel(own_ref, gram_ref, *refs):
    messages, (out_ref, total_ref) = refs[:-2], refs[-2:]
    width = own_ref.shape[1]
    total, gram = own_ref[...], gram_ref[...]
    for ref in messages:
        total = total + ref[:, :width].astype(jnp.float32)
        gram = gram + get_gram(ref, width, GRAM)
    out_ref[...] = total
    total_ref[...] = gram


def put_vector(vector, gram, plain_ref, wide_ref):
    rounded = vector.astype(jnp.bfloat16)
    width = vector.shape[1]
    plain_ref[...] = rounded
    wide_ref[:, :width] = rounded
    put_gram(wide_ref, width, gram)


def first_kernel(vector_ref, diagonal_ref, plain_ref, wide_ref):
    vector = vector_ref[...]
    gram = contract(vector, vector, ((1,), (1,)), HIGHEST)
    weighted = jnp.sum(vector * vector * diagonal_ref[...], axis=1, keepdims=True)
    gram = jnp.concatenate([gram, jnp.broadcast_to(weighted, gram.shape)], axis=1)
    put_vector(vector, gram, plain_ref, wide_ref)


def off_diagonal(refs):
    width = refs[0].shape[1]
    total = refs[0][...] + refs[1][...]
    for ref in refs[2:]:
        total = total + ref[:, :width].astype(jnp.float32)
    return total


def shift_kernel(gram_ref, shift_ref):
    gram = gram_ref[...]
    cases = gram.shape[0]
    norm = jnp.sum(identity(cases) * gram[:, :cases], keepdims=True)
    quotient = jnp.sum(gram[:, cases : cases + 1], keepdims=True) / norm
    shift_ref[...] = jnp.broadcast_to(quotient, shift_ref.shape)


def combine_kernel(vector_ref, diagonal_ref, shift_ref, *refs):
    sums, (next_ref, plain_ref, wide_ref) = refs[:-3], refs[-3:]
    vector = vector_ref[...]
    shift = shift_ref[0:1, 0:1]
    following = (diagonal_ref[...] - shift) * vector + off_diagonal(sums)
    next_ref[...] = following
    cross = contract(vector, following, ((1,), (1,)), HIGHEST)
    square = contract(following, following, ((1,), (1,)), HIGHEST)
    put_vector(following, jnp.concatenate([cross, square], axis=1), plain_ref, wide_ref)


def last_gram_kernel(both_ref, *refs):
    messages, total_ref = refs[:-1], refs[-1]
    cases = both_ref.shape[0]
    total = both_ref[...]
    for ref in messages:
        total = total + get_gram(ref, ref.shape[1] - PIECES * cases, cases)
    total_ref[...] = total


def solve(*pairs, panel=8):
    size = pairs[0][0].shape[0]
    works = [jnp.concatenate(pair, axis=1) for pair in pairs]
    shape = works[0].shape
    row = lax.broadcasted_iota(jnp.int32, shape, 0)
    for start in range(0, size, panel):
        pivots = range(start, start + panel)
        spread = [[jnp.broadcast_to(w[:, k : k + 1], shape) for k in pivots] for w in works]
        for k in pivots:
            for n, columns in enumerate(spread):
                pivot = columns[0]
                inverse = 1.0 / pivot[k : k + 1, :]

                def eliminate(matrix):
                    pivot_row = matrix[k : k + 1, :] * inverse
                    return jnp.where(row == k, pivot_row, matrix - pivot * pivot_row)

                works[n] = eliminate(works[n])
                spread[n] = [eliminate(column) for column in columns[1:]]
    return [work[:, size:] for work in works]


def identity(size):
    row = lax.broadcasted_iota(jnp.int32, (size, size), 0)
    column = lax.broadcasted_iota(jnp.int32, (size, size), 1)
    return jnp.where(row == column, 1.0, 0.0)


def first_coefficients_kernel(shift_ref, gram0_ref, gram1_ref, out_ref):
    cases = gram0_ref.shape[0]
    shift = shift_ref[0:1, 0:1]
    bb = gram0_ref[:, :cases]
    bu, uu = gram1_ref[:, :cases], gram1_ref[:, cases:]
    one = identity(cases)
    alpha0, inverse = solve((shift * bb + symmetric(bu), bb), (bb, one))
    r_b = one - shift * alpha0
    r = jnp.concatenate([r_b, -alpha0], axis=0)
    gram = jnp.concatenate(
        [jnp.concatenate([bb, bu], axis=1), jnp.concatenate([bu.T, uu], axis=1)], axis=0
    )
    rr1 = symmetric(mul_t(r, mul(gram, r)))
    d_b = r_b + mul(inverse, rr1)
    out_ref[...] = jnp.concatenate([alpha0, rr1, r_b, d_b], axis=1)


def stack(*parts):
    return jnp.concatenate(parts, axis=0)


def side(*parts):
    return jnp.concatenate(parts, axis=1)


def basis_gram(gram0_ref, gram1_ref, gram2_ref):
    cases = gram0_ref.shape[0]
    bb = gram0_ref[:, :cases]
    bu, uu = gram1_ref[:, :cases], gram1_ref[:, cases:]
    uv, vv = gram2_ref[:, :cases], gram2_ref[:, cases:]
    return stack(side(bb, bu, uu), side(bu.T, uu, uv), side(uu, uv.T, vv))


def directions(shift_ref, first_ref):
    cases = first_ref.shape[0]
    shift = shift_ref[0:1, 0:1]
    alpha0, _, r_b, d_b = [first_ref[:, k * cases : (k + 1) * cases] for k in range(4)]
    zero = jnp.zeros_like(alpha0)
    r1 = stack(r_b, -alpha0, zero)
    d1 = stack(d_b, -alpha0, zero)
    return r1, d1, stack(shift * d_b, d_b - shift * alpha0, -alpha0)


def second_solve_kernel(shift_ref, gram0_ref, gram1_ref, gram2_ref, first_ref, out_ref):
    cases = first_ref.shape[0]
    gram = basis_gram(gram0_ref, gram1_ref, gram2_ref)
    rr1 = first_ref[:, cases : 2 * cases]
    _, d1, s1 = directions(shift_ref, first_ref)
    curvature1 = symmetric(mul_t(d1, mul(gram, s1)))
    out_ref[...] = side(*solve((curvature1, rr1), (rr1, identity(cases))))


def second_coefficients_kernel(
    shift_ref, gram0_ref, gram1_ref, gram2_ref, first_ref, solve_ref, big_ref, small_ref
):
    cases = first_ref.shape[0]
    shift = shift_ref[0:1, 0:1]
    gram = basis_gram(gram0_ref, gram1_ref, gram2_ref)
    r1, d1, s1 = directions(shift_ref, first_ref)
    alpha1, inverse = solve_ref[:, :cases], solve_ref[:, cases:]
    uu = gram1_ref[:, cases:]
    uv, vv = gram2_ref[:, :cases], gram2_ref[:, cases:]
    r2 = r1 - mul(s1, alpha1)
    rr2 = symmetric(mul_t(r2, mul(gram, r2)))
    d2 = r2 + mul(d1, mul(inverse, rr2))
    d2_b, d2_u, d2_v = d2[:cases], d2[cases : 2 * cases], d2[2 * cases :]
    s2 = stack(shift * d2_b, d2_b + shift * d2_u, d2_u)
    with_y = mul_t(d2_b, uv + shift * uu) + mul_t(d2_u, vv + shift * uv)
    curvature2 = mul_t(d2, mul(gram, s2)) + mul(with_y, d2_v)
    zero = jnp.zeros_like(uu)
    x2 = stack(first_ref[:, :cases], zero, zero) + mul(d1, alpha1)
    small_ref[...] = side(curvature2, rr2, d2_v, zero)
    big_ref[...] = side(d2, r2, s2, x2)


def vectors_kernel(big_ref, b_ref, u_ref, v_ref, vectors_ref):
    basis = jnp.concatenate([b_ref[...], u_ref[...], v_ref[...]], axis=0)
    vectors_ref[...] = mul_t(big_ref[...], basis)


def finish_kernel(vectors_ref, small_ref, both_ref, other_ref, v_ref, diagonal_ref, *refs):
    sums, (solution_ref, residual_ref) = refs[:-2], refs[-2:]
    cases = v_ref.shape[0]
    d2, r2, s2, x2 = [vectors_ref[k * cases : (k + 1) * cases, :] for k in range(4)]
    curvature2, rr2, d2_v = [small_ref[:, k * cases : (k + 1) * cases] for k in range(3)]
    both = symmetric(both_ref[...] + other_ref[...])
    curvature2 = symmetric(curvature2 + mul_t(d2_v, mul(both, d2_v)))
    (alpha2,) = solve((curvature2, rr2), panel=16)
    y = diagonal_ref[...] * v_ref[...] + off_diagonal(sums)
    s2 = s2 + mul_t(d2_v, y)
    solution_ref[...] = x2 + mul_t(alpha2, d2)
    residual_ref[...] = r2 - mul_t(alpha2, s2)


def call(kernel, name, outs, *args, scratch=(), scalars=(), cost=0):
    return pl.pallas_call(
        kernel,
        out_shape=outs,
        in_specs=[smem if k in scalars else vmem for k in range(len(args))],
        out_specs=jax.tree.map(lambda _: vmem, outs),
        scratch_shapes=list(scratch),
        compiler_params=pltpu.CompilerParams(vmem_limit_bytes=VMEM_BYTES),
        cost_estimate=pl.CostEstimate(flops=int(cost * 1e9), bytes_accessed=0, transcendentals=0),
        name=name,
    )(*args)


def local(
    right_side,
    self_term,
    near_tiles,
    near_rows,
    near_cols,
    near_count,
    far_left,
    far_right,
    far_rows,
    far_cols,
    far_rank,
):
    cases, width = right_side.shape
    leaf = near_tiles.shape[-1]
    per = width // leaf
    rows, cols = lax.axis_size("row"), lax.axis_size("col")
    chips = cols // 2
    slots = near_tiles.shape[2] + far_left.shape[2]
    long = width + PIECES * GRAM
    table = jnp.concatenate(
        [
            jnp.stack([lax.axis_index("row"), lax.axis_index("col")]).astype(jnp.int32),
            near_rows[0, 0],
            far_rows[0, 0],
            near_cols[0, 0],
            far_cols[0, 0],
            far_rank[0, 0],
            near_count[0],
        ]
    )
    diagonal = self_term[None, :]
    tiles, turned = call(
        dense_kernel,
        "dense_tiles",
        [bf16(slots, leaf, leaf)] * 2,
        table,
        near_tiles[0, 0],
        far_left[0, 0],
        far_right[0, 0],
        scalars=(0,),
    )

    def apply(plain, wide, during, last=()):
        over_row = [partner_permute(wide, "row", k) for k in range(1, rows)]
        held, flip = {0: plain}, chips // 2
        while flip:
            held |= {k ^ flip: partner_permute(m, "col", 2 * flip) for k, m in held.items()}
            flip //= 2
        over_chip = [held[k] for k in range(1, chips)]
        send, keep, gram = call(
            rows_kernel,
            "rows_half",
            [bf16(chips + 1, cases, width), f32(chips, cases, width), f32(cases, GRAM)],
            table,
            turned,
            wide,
            *over_row,
            scalars=(0,),
            scratch=[
                pltpu.VMEM((rows * per, cases, leaf), jnp.bfloat16),
                pltpu.VMEM((cols * per, cases, leaf), jnp.float32),
            ],
        )
        over_chip, send, keep = lax.optimization_barrier((over_chip, send, keep))
        got = partner_permute(send, "col", 1)
        other_core = [partner_permute(v, "col", 1) for v in [plain] + over_chip]
        got, other_core = lax.optimization_barrier((got, other_core))
        own_chip, gram, *row_messages = call(
            pair_kernel,
            "pair_sums",
            [f32(cases, width), f32(cases, GRAM)] + [bf16(cases, long)] * (chips - 1),
            table,
            keep,
            gram,
            got,
            scalars=(0,),
        )
        from_chips = [partner_permute(m, "col", 2 * k) for k, m in enumerate(row_messages, 1)]
        own_row, gram = call(
            chip_sums_kernel,
            "chip_sums",
            [f32(cases, width), f32(cases, GRAM)],
            own_chip,
            gram,
            *from_chips,
            cost=1,
        )
        row_group = [None] * cols
        for k, (a, b) in enumerate(zip([plain] + over_chip, other_core)):
            row_group[2 * k], row_group[2 * k + 1] = a, b
        behind = PIECES * cases if last else 0
        own_col, *outs = call(
            functools.partial(cols_kernel, rows, cols),
            "cols_half",
            [f32(cases, width)]
            + [bf16(cases, width + behind)] * (rows - 1)
            + [f32(cases, cases)] * bool(last),
            table,
            tiles,
            *row_group,
            *([wide, *over_row, *last] if last else []),
            scalars=(0,),
            scratch=[
                pltpu.VMEM((cols * per, cases, leaf), jnp.bfloat16),
                pltpu.VMEM((rows * per, cases, leaf), jnp.float32),
            ],
        )
        from_rows = [partner_permute(m, "row", k) for k, m in enumerate(outs[: rows - 1], 1)]
        made = during(gram)
        from_rows, made = lax.optimization_barrier((from_rows, made))
        sums = [own_row, own_col, *from_rows]
        if not last:
            return sums, gram, made
        both = call(last_gram_kernel, "last_gram", f32(cases, cases), outs[-1], *from_rows)
        return sums, gram, made, both

    def advance(vector, shift, sums):
        return call(
            combine_kernel,
            "combine",
            [f32(cases, width), bf16(cases, width), bf16(cases, long)],
            vector,
            diagonal,
            shift,
            *sums,
        )

    b = right_side
    plain, wide = call(
        first_kernel, "first_message", [bf16(cases, width), bf16(cases, long)], b, diagonal, cost=10
    )
    sums, gram0, shift = apply(
        plain, wide, lambda gram: call(shift_kernel, "shift", f32(8, 128), gram)
    )
    u, plain, wide = advance(b, shift, sums)
    sums, gram1, first = apply(
        plain,
        wide,
        lambda gram: call(
            first_coefficients_kernel, "coefficients", f32(cases, 4 * cases), shift, gram0, gram
        ),
    )
    v, plain, wide = advance(u, shift, sums)
    sums, gram2, solved, both = apply(
        plain,
        wide,
        lambda gram: call(
            second_solve_kernel, "solve", f32(cases, 2 * cases), shift, gram0, gram1, gram, first
        ),
        last=(v, diagonal),
    )
    over_chip = [partner_permute(both, "col", 2 * k) for k in range(1, chips)]
    big, small = call(
        second_coefficients_kernel,
        "coefficients",
        [f32(3 * cases, 4 * cases), f32(cases, 4 * cases)],
        shift,
        gram0,
        gram1,
        gram2,
        first,
        solved,
    )
    over_chip, big = lax.optimization_barrier((over_chip, big))
    both = functools.reduce(jnp.add, over_chip, both)
    other = partner_permute(both, "col", 1)
    big, _ = lax.optimization_barrier((big, both))
    vectors = call(vectors_kernel, "vectors", f32(4 * cases, width), big, b, u, v)
    other, vectors = lax.optimization_barrier((other, vectors))
    return call(
        finish_kernel,
        "finish",
        [f32(cases, width), f32(cases, width)],
        vectors,
        small,
        both,
        other,
        v,
        diagonal,
        *sums,
    )


def solution(mesh):
    in_specs = (
        P(None, ("row", "col")),
        P(("row", "col")),
        P("row", "col", None, None, None),
        P("row", "col", None),
        P("row", "col", None),
        P("row", "col"),
        P("row", "col", None, None, None),
        P("row", "col", None, None, None),
        P("row", "col", None),
        P("row", "col", None),
        P("row", "col", None),
    )
    out_specs = (P(None, ("row", "col")), P(None, ("row", "col")))
    return jax.shard_map(local, mesh=mesh, in_specs=in_specs, out_specs=out_specs, check_vma=False)
```

```python
import functools

import jax
import jax.numpy as jnp
from jax import lax
from jax.experimental import pallas as pl
from jax.experimental.pallas import tpu as pltpu
from jax.sharding import PartitionSpec as P

VMEM_BYTES = 24 * 1024 * 1024
HIGHEST = lax.Precision.HIGHEST
GRAM = 128
PIECES = 2
UNROLL = 96

vmem = pl.BlockSpec(memory_space=pltpu.VMEM)
smem = pl.BlockSpec(memory_space=pltpu.SMEM)


def f32(*shape):
    return jax.ShapeDtypeStruct(shape, jnp.float32)


def bf16(*shape):
    return jax.ShapeDtypeStruct(shape, jnp.bfloat16)


def contract(left, right, dims, precision=None):
    return lax.dot_general(
        left, right, (dims, ((), ())), precision=precision, preferred_element_type=jnp.float32
    )


def mul(left, right):
    return contract(left, right, ((1,), (0,)), HIGHEST)


def mul_t(left, right):
    return contract(left, right, ((0,), (0,)), HIGHEST)


def symmetric(matrix):
    return 0.5 * (matrix + matrix.T)


def partner_permute(value, axis, flip):
    size = lax.axis_size(axis)
    return lax.ppermute(value, axis, [(i, i ^ flip) for i in range(size)])


def put_gram(ref, first, gram):
    columns = gram.shape[1]
    for k in range(PIECES):
        piece = gram.astype(jnp.bfloat16)
        ref[:, first + k * columns : first + (k + 1) * columns] = piece
        gram = gram - piece.astype(jnp.float32)


def get_gram(ref, first, columns):
    parts = [
        ref[:, first + k * columns : first + (k + 1) * columns].astype(jnp.float32)
        for k in range(PIECES)
    ]
    return functools.reduce(jnp.add, reversed(parts))


def dense_kernel(table, near_ref, left_ref, right_ref, tile_ref, turned_ref):
    near_slots, far_slots = near_ref.shape[0], left_ref.shape[0]
    ranks = 2 + 2 * (near_slots + far_slots)
    count = table[ranks + far_slots]

    def far(s, _):
        row = lax.broadcasted_iota(jnp.int32, left_ref.shape[1:], 0)
        left = jnp.where(row < table[ranks + s], left_ref[s].astype(jnp.float32), 0.0)
        left, right = left.astype(jnp.bfloat16), right_ref[s]
        tile_ref[near_slots + s] = contract(left, right, ((0,), (0,))).astype(jnp.bfloat16)
        turned_ref[near_slots + s] = contract(right, left, ((0,), (0,))).astype(jnp.bfloat16)
        return 0

    def near(s, _):
        tile = near_ref[s]
        tile = jnp.where(s < count, tile, jnp.zeros_like(tile))
        tile_ref[s] = tile
        turned_ref[s] = tile.T
        return 0

    lax.fori_loop(0, far_slots, far, 0, unroll=16)
    lax.fori_loop(0, near_slots, near, 0, unroll=8)


def tile_sums(table, inputs, outputs, tile_ref, cells, total):
    total[...] = jnp.zeros_like(total)

    def step(s, _):
        product = contract(cells[table[inputs + s]], tile_ref[s], ((1,), (0,)))
        to = table[outputs + s]
        total[to] = total[to] + product
        return 0

    lax.fori_loop(0, tile_ref.shape[0], step, 0, unroll=UNROLL)


def place(block, ref, cells, per):
    leaf = cells.shape[-1]
    for j in range(per):
        cells[block * per + j] = ref[:, j * leaf : (j + 1) * leaf]


def rows_kernel(table, tile_ref, *refs):
    blocks, (send_ref, keep_ref, gram_ref, cells, total) = refs[:-5], refs[-5:]
    chips, _, width = keep_ref.shape
    leaf = cells.shape[-1]
    per = width // leaf
    me, core = table[0], table[1] % 2
    for flip, ref in enumerate(blocks):
        place(me ^ flip, ref, cells, per)
    slots = tile_ref.shape[0]
    tile_sums(table, 2 + slots, 2, tile_ref, cells, total)
    for z in range(chips):
        for j in range(per):
            part = slice(j * leaf, (j + 1) * leaf)
            send_ref[z, :, part] = total[(2 * z + 1 - core) * per + j].astype(jnp.bfloat16)
            keep_ref[z, :, part] = total[(2 * z + core) * per + j]
    gram = functools.reduce(jnp.add, [get_gram(ref, width, GRAM) for ref in blocks])
    gram_ref[...] = gram
    send_ref[chips] = jnp.zeros(send_ref.shape[1:], send_ref.dtype)
    put_gram(send_ref.at[chips], 0, gram)


def cols_kernel(rows, cols, table, tile_ref, *refs):
    blocks, refs, (cells, total) = refs[:cols], refs[cols:-2], refs[-2:]
    last = refs[: rows + 1] if len(refs) > rows else ()
    outs = refs[len(last) : len(last) + rows]
    width = outs[0].shape[1]
    leaf = cells.shape[-1]
    per = width // leaf
    me = table[0]
    for flip, ref in enumerate(blocks):
        place(table[1] ^ flip, ref, cells, per)
    slots = tile_ref.shape[0]
    tile_sums(table, 2, 2 + slots, tile_ref, cells, total)
    for flip, out in enumerate(outs):
        for j in range(per):
            part = total[(me ^ flip) * per + j]
            out[:, j * leaf : (j + 1) * leaf] = part.astype(out.dtype)
    if last:
        both = last[rows][...]
        half = jnp.zeros_like(both)
        for flip, ref in enumerate(last[:rows]):
            for j in range(per):
                cluster = ref[:, j * leaf : (j + 1) * leaf]
                image = total[(me ^ flip) * per + j].astype(jnp.bfloat16)
                half = half + contract(cluster, image, ((1,), (1,)))
        both = both + 2.0 * half
        refs[-1][...] = both
        for out in outs[1:]:
            put_gram(out, width, both)


def pair_kernel(table, keep_ref, gram_ref, got_ref, own_ref, own_gram_ref, *messages):
    chips, _, width = keep_ref.shape
    chip = table[1] // 2
    gram = gram_ref[...] + get_gram(got_ref.at[chips], 0, GRAM)
    own_gram_ref[...] = gram
    for flip, out in enumerate((own_ref, *messages)):
        z = chip ^ flip
        out[:, :width] = (keep_ref[z] + got_ref[z].astype(jnp.float32)).astype(out.dtype)
    for out in messages:
        put_gram(out, width, gram)


def chip_sums_kernel(own_ref, gram_ref, *refs):
    messages, (out_ref, total_ref) = refs[:-2], refs[-2:]
    width = own_ref.shape[1]
    total, gram = own_ref[...], gram_ref[...]
    for ref in messages:
        total = total + ref[:, :width].astype(jnp.float32)
        gram = gram + get_gram(ref, width, GRAM)
    out_ref[...] = total
    total_ref[...] = gram


def put_vector(vector, gram, plain_ref, wide_ref):
    rounded = vector.astype(jnp.bfloat16)
    width = vector.shape[1]
    plain_ref[...] = rounded
    wide_ref[:, :width] = rounded
    put_gram(wide_ref, width, gram)


def first_kernel(vector_ref, diagonal_ref, plain_ref, wide_ref):
    vector = vector_ref[...]
    gram = contract(vector, vector, ((1,), (1,)), HIGHEST)
    weighted = jnp.sum(vector * vector * diagonal_ref[...], axis=1, keepdims=True)
    gram = jnp.concatenate([gram, jnp.broadcast_to(weighted, gram.shape)], axis=1)
    put_vector(vector, gram, plain_ref, wide_ref)


def off_diagonal(refs):
    width = refs[0].shape[1]
    total = refs[0][...] + refs[1][...]
    for ref in refs[2:]:
        total = total + ref[:, :width].astype(jnp.float32)
    return total


def shift_kernel(gram_ref, shift_ref):
    gram = gram_ref[...]
    cases = gram.shape[0]
    norm = jnp.sum(identity(cases) * gram[:, :cases], keepdims=True)
    quotient = jnp.sum(gram[:, cases : cases + 1], keepdims=True) / norm
    shift_ref[...] = jnp.broadcast_to(quotient, shift_ref.shape)


def combine_kernel(vector_ref, diagonal_ref, shift_ref, *refs):
    sums, (next_ref, plain_ref, wide_ref) = refs[:-3], refs[-3:]
    vector = vector_ref[...]
    shift = shift_ref[0:1, 0:1]
    following = (diagonal_ref[...] - shift) * vector + off_diagonal(sums)
    next_ref[...] = following
    cross = contract(vector, following, ((1,), (1,)), HIGHEST)
    square = contract(following, following, ((1,), (1,)), HIGHEST)
    put_vector(following, jnp.concatenate([cross, square], axis=1), plain_ref, wide_ref)


def weighted_kernel(vector_ref, diagonal_ref, out_ref):
    vector = vector_ref[...]
    out_ref[...] = contract(vector, vector * diagonal_ref[...], ((1,), (1,)), HIGHEST)


def last_gram_kernel(both_ref, *refs):
    messages, total_ref = refs[:-1], refs[-1]
    cases = both_ref.shape[0]
    total = both_ref[...]
    for ref in messages:
        total = total + get_gram(ref, ref.shape[1] - PIECES * cases, cases)
    total_ref[...] = total


def solve(*pairs, panel=8):
    size = pairs[0][0].shape[0]
    works = [jnp.concatenate(pair, axis=1) for pair in pairs]
    shape = works[0].shape
    row = lax.broadcasted_iota(jnp.int32, shape, 0)
    for start in range(0, size, panel):
        pivots = range(start, start + panel)
        spread = [[jnp.broadcast_to(w[:, k : k + 1], shape) for k in pivots] for w in works]
        for k in pivots:
            for n, columns in enumerate(spread):
                pivot = columns[0]
                inverse = 1.0 / pivot[k : k + 1, :]

                def eliminate(matrix):
                    pivot_row = matrix[k : k + 1, :] * inverse
                    return jnp.where(row == k, pivot_row, matrix - pivot * pivot_row)

                works[n] = eliminate(works[n])
                spread[n] = [eliminate(column) for column in columns[1:]]
    return [work[:, size:] for work in works]


def identity(size):
    row = lax.broadcasted_iota(jnp.int32, (size, size), 0)
    column = lax.broadcasted_iota(jnp.int32, (size, size), 1)
    return jnp.where(row == column, 1.0, 0.0)


def first_coefficients_kernel(shift_ref, gram0_ref, gram1_ref, out_ref):
    cases = gram0_ref.shape[0]
    shift = shift_ref[0:1, 0:1]
    bb = gram0_ref[:, :cases]
    bu, uu = gram1_ref[:, :cases], gram1_ref[:, cases:]
    one = identity(cases)
    alpha0, inverse = solve((shift * bb + symmetric(bu), bb), (bb, one))
    r_b = one - shift * alpha0
    r = jnp.concatenate([r_b, -alpha0], axis=0)
    gram = jnp.concatenate(
        [jnp.concatenate([bb, bu], axis=1), jnp.concatenate([bu.T, uu], axis=1)], axis=0
    )
    rr1 = symmetric(mul_t(r, mul(gram, r)))
    d_b = r_b + mul(inverse, rr1)
    out_ref[...] = jnp.concatenate([alpha0, rr1, r_b, d_b], axis=1)


def stack(*parts):
    return jnp.concatenate(parts, axis=0)


def side(*parts):
    return jnp.concatenate(parts, axis=1)


def basis_gram(gram0_ref, gram1_ref, gram2_ref):
    cases = gram0_ref.shape[0]
    bb = gram0_ref[:, :cases]
    bu, uu = gram1_ref[:, :cases], gram1_ref[:, cases:]
    uv, vv = gram2_ref[:, :cases], gram2_ref[:, cases:]
    return stack(side(bb, bu, uu), side(bu.T, uu, uv), side(uu, uv.T, vv))


def directions(shift_ref, first_ref):
    cases = first_ref.shape[0]
    shift = shift_ref[0:1, 0:1]
    alpha0, _, r_b, d_b = [first_ref[:, k * cases : (k + 1) * cases] for k in range(4)]
    zero = jnp.zeros_like(alpha0)
    r1 = stack(r_b, -alpha0, zero)
    d1 = stack(d_b, -alpha0, zero)
    return r1, d1, stack(shift * d_b, d_b - shift * alpha0, -alpha0)


def second_solve_kernel(shift_ref, gram0_ref, gram1_ref, gram2_ref, first_ref, out_ref):
    cases = first_ref.shape[0]
    gram = basis_gram(gram0_ref, gram1_ref, gram2_ref)
    rr1 = first_ref[:, cases : 2 * cases]
    _, d1, s1 = directions(shift_ref, first_ref)
    curvature1 = symmetric(mul_t(d1, mul(gram, s1)))
    out_ref[...] = side(*solve((curvature1, rr1), (rr1, identity(cases))))


def second_coefficients_kernel(
    shift_ref, gram0_ref, gram1_ref, gram2_ref, first_ref, solve_ref, big_ref, small_ref
):
    cases = first_ref.shape[0]
    shift = shift_ref[0:1, 0:1]
    gram = basis_gram(gram0_ref, gram1_ref, gram2_ref)
    r1, d1, s1 = directions(shift_ref, first_ref)
    alpha1, inverse = solve_ref[:, :cases], solve_ref[:, cases:]
    uu = gram1_ref[:, cases:]
    uv, vv = gram2_ref[:, :cases], gram2_ref[:, cases:]
    r2 = r1 - mul(s1, alpha1)
    rr2 = symmetric(mul_t(r2, mul(gram, r2)))
    d2 = r2 + mul(d1, mul(inverse, rr2))
    d2_b, d2_u, d2_v = d2[:cases], d2[cases : 2 * cases], d2[2 * cases :]
    s2 = stack(shift * d2_b, d2_b + shift * d2_u, d2_u)
    with_y = mul_t(d2_b, uv + shift * uu) + mul_t(d2_u, vv + shift * uv)
    curvature2 = mul_t(d2, mul(gram, s2)) + mul(with_y, d2_v)
    zero = jnp.zeros_like(uu)
    x2 = stack(first_ref[:, :cases], zero, zero) + mul(d1, alpha1)
    small_ref[...] = side(curvature2, rr2, d2_v, zero)
    big_ref[...] = side(d2, r2, s2, x2)


def vectors_kernel(big_ref, b_ref, u_ref, v_ref, vectors_ref):
    basis = jnp.concatenate([b_ref[...], u_ref[...], v_ref[...]], axis=0)
    vectors_ref[...] = mul_t(big_ref[...], basis)


def finish_kernel(vectors_ref, small_ref, both_ref, other_ref, v_ref, diagonal_ref, *refs):
    sums, (solution_ref, residual_ref) = refs[:-2], refs[-2:]
    cases = v_ref.shape[0]
    d2, r2, s2, x2 = [vectors_ref[k * cases : (k + 1) * cases, :] for k in range(4)]
    curvature2, rr2, d2_v = [small_ref[:, k * cases : (k + 1) * cases] for k in range(3)]
    both = symmetric(both_ref[...] + other_ref[...])
    curvature2 = symmetric(curvature2 + mul_t(d2_v, mul(both, d2_v)))
    (alpha2,) = solve((curvature2, rr2), panel=16)
    y = diagonal_ref[...] * v_ref[...] + off_diagonal(sums)
    s2 = s2 + mul_t(d2_v, y)
    solution_ref[...] = x2 + mul_t(alpha2, d2)
    residual_ref[...] = r2 - mul_t(alpha2, s2)


def call(kernel, name, outs, *args, scratch=(), scalars=(), cost=0):
    return pl.pallas_call(
        kernel,
        out_shape=outs,
        in_specs=[smem if k in scalars else vmem for k in range(len(args))],
        out_specs=jax.tree.map(lambda _: vmem, outs),
        scratch_shapes=list(scratch),
        compiler_params=pltpu.CompilerParams(vmem_limit_bytes=VMEM_BYTES),
        cost_estimate=pl.CostEstimate(flops=int(cost * 1e9), bytes_accessed=0, transcendentals=0),
        name=name,
    )(*args)


def local(
    right_side,
    self_term,
    near_tiles,
    near_rows,
    near_cols,
    near_count,
    far_left,
    far_right,
    far_rows,
    far_cols,
    far_rank,
):
    cases, width = right_side.shape
    leaf = near_tiles.shape[-1]
    per = width // leaf
    rows, cols = lax.axis_size("row"), lax.axis_size("col")
    chips = cols // 2
    slots = near_tiles.shape[2] + far_left.shape[2]
    long = width + PIECES * GRAM
    table = jnp.concatenate(
        [
            jnp.stack([lax.axis_index("row"), lax.axis_index("col")]).astype(jnp.int32),
            near_rows[0, 0],
            far_rows[0, 0],
            near_cols[0, 0],
            far_cols[0, 0],
            far_rank[0, 0],
            near_count[0],
        ]
    )
    diagonal = self_term[None, :]
    tiles, turned = call(
        dense_kernel,
        "dense_tiles",
        [bf16(slots, leaf, leaf)] * 2,
        table,
        near_tiles[0, 0],
        far_left[0, 0],
        far_right[0, 0],
        scalars=(0,),
    )

    def apply(plain, wide, during, last=()):
        over_row = [partner_permute(wide, "row", k) for k in range(1, rows)]
        held, flip = {0: plain}, chips // 2
        while flip:
            held |= {k ^ flip: partner_permute(m, "col", 2 * flip) for k, m in held.items()}
            flip //= 2
        over_chip = [held[k] for k in range(1, chips)]
        held_wide = wide
        if last:
            weighted = call(weighted_kernel, "weighted", f32(cases, cases), *last)
            held_wide, weighted = lax.optimization_barrier((wide, weighted))
        send, keep, gram = call(
            rows_kernel,
            "rows_half",
            [bf16(chips + 1, cases, width), f32(chips, cases, width), f32(cases, GRAM)],
            table,
            turned,
            held_wide,
            *over_row,
            scalars=(0,),
            scratch=[
                pltpu.VMEM((rows * per, cases, leaf), jnp.bfloat16),
                pltpu.VMEM((cols * per, cases, leaf), jnp.float32),
            ],
        )
        over_chip, send, keep = lax.optimization_barrier((over_chip, send, keep))
        got = partner_permute(send, "col", 1)
        other_core = [partner_permute(v, "col", 1) for v in [plain] + over_chip]
        got, other_core = lax.optimization_barrier((got, other_core))
        own_chip, gram, *row_messages = call(
            pair_kernel,
            "pair_sums",
            [f32(cases, width), f32(cases, GRAM)] + [bf16(cases, long)] * (chips - 1),
            table,
            keep,
            gram,
            got,
            scalars=(0,),
        )
        from_chips = [partner_permute(m, "col", 2 * k) for k, m in enumerate(row_messages, 1)]
        own_row, gram = call(
            chip_sums_kernel,
            "chip_sums",
            [f32(cases, width), f32(cases, GRAM)],
            own_chip,
            gram,
            *from_chips,
            cost=1,
        )
        row_group = [None] * cols
        for k, (a, b) in enumerate(zip([plain] + over_chip, other_core)):
            row_group[2 * k], row_group[2 * k + 1] = a, b
        behind = PIECES * cases if last else 0
        own_col, *outs = call(
            functools.partial(cols_kernel, rows, cols),
            "cols_half",
            [f32(cases, width)]
            + [bf16(cases, width + behind)] * (rows - 1)
            + [f32(cases, cases)] * bool(last),
            table,
            tiles,
            *row_group,
            *([held_wide, *over_row, weighted] if last else []),
            scalars=(0,),
            scratch=[
                pltpu.VMEM((cols * per, cases, leaf), jnp.bfloat16),
                pltpu.VMEM((rows * per, cases, leaf), jnp.float32),
            ],
        )
        from_rows = [partner_permute(m, "row", k) for k, m in enumerate(outs[: rows - 1], 1)]
        made = during(gram)
        from_rows, made = lax.optimization_barrier((from_rows, made))
        sums = [own_row, own_col, *from_rows]
        if not last:
            return sums, gram, made
        both = call(last_gram_kernel, "last_gram", f32(cases, cases), outs[-1], *from_rows)
        return sums, gram, made, both

    def advance(vector, shift, sums):
        return call(
            combine_kernel,
            "combine",
            [f32(cases, width), bf16(cases, width), bf16(cases, long)],
            vector,
            diagonal,
            shift,
            *sums,
        )

    b = right_side
    plain, wide = call(
        first_kernel, "first_message", [bf16(cases, width), bf16(cases, long)], b, diagonal, cost=10
    )
    sums, gram0, shift = apply(
        plain, wide, lambda gram: call(shift_kernel, "shift", f32(8, 128), gram)
    )
    u, plain, wide = advance(b, shift, sums)
    sums, gram1, first = apply(
        plain,
        wide,
        lambda gram: call(
            first_coefficients_kernel, "coefficients", f32(cases, 4 * cases), shift, gram0, gram
        ),
    )
    v, plain, wide = advance(u, shift, sums)
    sums, gram2, solved, both = apply(
        plain,
        wide,
        lambda gram: call(
            second_solve_kernel, "solve", f32(cases, 2 * cases), shift, gram0, gram1, gram, first
        ),
        last=(v, diagonal),
    )
    over_chip = [partner_permute(both, "col", 2 * k) for k in range(1, chips)]
    big, small = call(
        second_coefficients_kernel,
        "coefficients",
        [f32(3 * cases, 4 * cases), f32(cases, 4 * cases)],
        shift,
        gram0,
        gram1,
        gram2,
        first,
        solved,
    )
    over_chip, big = lax.optimization_barrier((over_chip, big))
    both = functools.reduce(jnp.add, over_chip, both)
    other = partner_permute(both, "col", 1)
    big, _ = lax.optimization_barrier((big, both))
    vectors = call(vectors_kernel, "vectors", f32(4 * cases, width), big, b, u, v)
    other, vectors = lax.optimization_barrier((other, vectors))
    return call(
        finish_kernel,
        "finish",
        [f32(cases, width), f32(cases, width)],
        vectors,
        small,
        both,
        other,
        v,
        diagonal,
        *sums,
    )


def solution(mesh):
    in_specs = (
        P(None, ("row", "col")),
        P(("row", "col")),
        P("row", "col", None, None, None),
        P("row", "col", None),
        P("row", "col", None),
        P("row", "col"),
        P("row", "col", None, None, None),
        P("row", "col", None, None, None),
        P("row", "col", None),
        P("row", "col", None),
        P("row", "col", None),
    )
    out_specs = (P(None, ("row", "col")), P(None, ("row", "col")))
    return jax.shard_map(local, mesh=mesh, in_specs=in_specs, out_specs=out_specs, check_vma=False)
```
